32 devices in a mesh: grp: 4 (over y, x), dev: 8 (over z, core).
Axes of the slice: x: 2, y: 2, z: 4, core: 2. Of those that a mesh axis runs over, the one named last changes fastest.
Arguments:
- embeds: bfloat16 [3072, 1024], P(('grp', 'dev')), may hold values from -6 to 6
- cluster: int32 [3072], P(('grp', 'dev')), may hold values from 0 to 7, as said below
- priority: int32 [3072], P(('grp', 'dev')), may hold values from 0 to 3071, each once
Outputs:
- best: float32 [3072], P(('grp', 'dev'))
The draws below stay inside these ranges and needn't reach their ends.
Inputs may be any that keep to these rules, and one draw needn't show every extreme that they name: `cluster`: cluster c belongs to group c // 2. Among the items of one device, at most 48 belong to the clusters of one group, and exactly 48 to some group. `priority`: each number appears once.
All inputs are finite; a program needn't handle non-finite values.
Results may differ from the reference program's by a relative error of at most 0.0013.
Values may be sent and summed in bfloat16 or wider, within the bound.
A program may use at most 128 MiB of HBM per device.

```python
import jax
import jax.numpy as jnp
from jax import lax

D = 1024
ITEM_DEV = 96
CLUST_GRP = 2
CAP = 48
ITEMS = 3072
N_GRP = 4
DEVICES = 32


def draw_cluster(key, part):
    subkeys = jax.random.split(key, 6)
    primary = jnp.minimum(jax.random.randint(subkeys[0], (DEVICES,), 0, N_GRP), jax.random.randint(subkeys[1], (DEVICES,), 0, N_GRP))
    offsets = jax.random.randint(subkeys[2], (DEVICES, ITEM_DEV - CAP), 1, N_GRP)
    others = (primary[:, None] + offsets) % N_GRP
    group_of = jnp.concatenate([jnp.broadcast_to(primary[:, None], (DEVICES, CAP)), others], axis=1)
    noise = jax.random.randint(subkeys[3], (DEVICES, ITEM_DEV), 0, 2 ** 20) * ITEM_DEV + jnp.arange(ITEM_DEV, dtype=jnp.int32)[None, :]
    shuffle = jnp.argsort(noise, axis=1, stable=True)
    group_of = jnp.take_along_axis(group_of, shuffle, axis=1)
    within = jnp.minimum(jax.random.randint(subkeys[4], (DEVICES, ITEM_DEV), 0, CLUST_GRP), jax.random.randint(subkeys[5], (DEVICES, ITEM_DEV), 0, CLUST_GRP))
    return (group_of * CLUST_GRP + within).reshape(-1).astype(jnp.int32)


def level_of(rng, dims, cuts, least, largest):
    def one(dim, parts):
        draws = jax.random.uniform(jax.random.fold_in(jax.random.fold_in(rng, 6), dim), (parts,), jnp.float32, least / len(cuts), largest / len(cuts))
        return jnp.repeat(jnp.exp(draws), dims[dim] // parts).reshape((-1,) + (1,) * (len(dims) - dim - 1))

    loudness = one(*cuts[0])
    for cut in cuts[1:]:
        loudness = loudness * one(*cut)
    return loudness


def bell_draw(stream_key, extent, width, bound, cuts=(), kind=jnp.bfloat16):
    level = level_of(stream_key, extent, cuts, -0.22, 0.18) if cuts else 1.0
    drawn = jax.random.normal(stream_key, extent, jnp.float32) * width * level
    return jnp.minimum(jnp.maximum(drawn, -bound), bound).astype(kind)


def setup_inputs(seed: int = 0) -> dict:
    splits = jax.random.split(jax.random.key(seed), 4)
    embeds = bell_draw(splits[0], (ITEMS, D), 1.0, 6.0, ((0, 32),))
    cluster = draw_cluster(jax.random.fold_in(splits[3], 71), 0)
    priority = jax.random.permutation(splits[2], ITEMS).astype(jnp.int32)
    return {"embeds": embeds, "cluster": cluster, "priority": priority}


def reference(embeds, cluster, priority):
    values = embeds.astype(jnp.float32)
    normed = (values * lax.rsqrt(lax.optimization_barrier(jnp.sum(values * values, axis=1, keepdims=True)) + 1e-06)).astype(jnp.bfloat16)
    block_rows = ITEM_DEV * 8

    def one_block(pieces):
        left, left_cluster, left_rank = pieces
        scores = jnp.dot(left, normed.T, preferred_element_type=jnp.float32)
        chosen = (left_cluster[:, None] == cluster[None, :]) & (priority[None, :] < left_rank[:, None])
        return lax.optimization_barrier(jnp.max(jnp.where(chosen, scores, -1.0), axis=1))
    result = lax.map(one_block, (normed.reshape(-1, block_rows, D), cluster.reshape(-1, block_rows), priority.reshape(-1, block_rows)))
    return result.reshape(-1)
```

```python
import functools

import jax
import jax.numpy as jnp
from jax import lax
from jax.experimental import pallas as pl
from jax.experimental.pallas import tpu as pltpu
from jax.sharding import PartitionSpec as P

MESH = pl.DeviceIdType.MESH
LANES = 128


def kernel(
    groups, layers, embeds_ref, cluster_ref, priority_ref, out_ref,
    plane, column, plane_key, column_key, plane_res, column_res, plane_got, column_got, total,
    plane_send, plane_recv, column_send, column_recv, pass_send, pass_recv,
    plane_key_send, plane_key_recv, column_key_send, column_key_recv,
    plane_res_send, plane_res_recv, column_res_send, column_res_recv,
):
    items, width = embeds_ref.shape
    lanes = plane.shape[1]
    g, d = lax.axis_index("grp"), lax.axis_index("dev")
    z, c = d // 2, d % 2

    def at(group, layer, core):
        return {"grp": group, "dev": layer * 2 + core}

    def group_up(s):
        return (g + s) % groups

    def group_down(s):
        return (g + groups - s) % groups

    def layer_up(s):
        return (z + s) % layers

    def layer_down(s):
        return (z + layers - s) % layers

    def core(k):
        return (c + k) % 2

    def sends(s):
        return (s % 2 == 0) & (z + s < layers) | (s % 2 == 1) & (z + s >= layers)

    def takes(s):
        return (s % 2 == 0) & (z >= s) | (s % 2 == 1) & (z < s)

    def remote(src, dst, send, recv, device):
        return pltpu.make_async_remote_copy(
            src_ref=src, dst_ref=dst, send_sem=send, recv_sem=recv,
            device_id=device, device_id_type=MESH,
        )

    def each(count, body):
        lax.fori_loop(1, count, lambda s, carry: (body(s), carry)[1], 0)

    def each_if(test, body):
        def step(s):
            pl.when(test(s))(lambda: body(s))
        each(layers, step)

    def plane_copy(s):
        return remote(plane.at[0, pl.ds(0, items)], plane.at[s, pl.ds(0, items)],
                      plane_send.at[s], plane_recv.at[s], at(group_up(s), z, c))

    def column_copy(s):
        return remote(column.at[0, 0], column.at[s, 0],
                      column_send.at[s], column_recv.at[s], at(g, layer_up(s), c))

    def pass_copy(s):
        return remote(column.at[s, 0], column.at[s, 1],
                      pass_send.at[s], pass_recv.at[s], at(g, z, core(1)))

    def plane_key_copy(s):
        return remote(plane_key.at[0], plane_key.at[s],
                      plane_key_send.at[s], plane_key_recv.at[s], at(group_up(s), z, c))

    def column_key_copy(s, k):
        return remote(column_key.at[0, 0], column_key.at[s, k],
                      column_key_send.at[s, k], column_key_recv.at[s, k], at(g, layer_up(s), core(k)))

    def plane_res_copy(s):
        return remote(plane_res.at[s], plane_got.at[s],
                      plane_res_send.at[s], plane_res_recv.at[s], at(group_down(s), z, c))

    def column_res_copy(s, k):
        return remote(column_res.at[s, k], column_got.at[s, k],
                      column_res_send.at[s, k], column_res_recv.at[s, k], at(g, layer_down(s), core(k)))

    barrier = pltpu.get_barrier_semaphore()

    def greet(device):
        pl.semaphore_signal(barrier, inc=1, device_id=device, device_id_type=MESH)

    def greet_layer(s):
        greet(at(g, layer_up(s), c))
        greet(at(g, layer_up(s), core(1)))

    each(groups, lambda s: greet(at(group_up(s), z, c)))
    greet(at(g, z, core(1)))
    each(layers, greet_layer)

    values = embeds_ref[...].astype(jnp.float32)
    normed = (values * lax.rsqrt(jnp.sum(values * values, axis=1, keepdims=True) + 1e-06)).astype(
        jnp.bfloat16
    )
    plane[0, :items] = normed
    column[0, 0] = normed
    if lanes > items:
        for s in range(groups):
            plane[s, items:] = jnp.zeros((lanes - items, width), jnp.bfloat16)
    key = jnp.full((8, lanes), -1, jnp.int32)
    plane_key[0] = key
    plane_key[0, 0:1, :items] = cluster_ref[...].reshape(1, items)
    plane_key[0, 1:2, :items] = priority_ref[...].reshape(1, items)
    column_key[0, 0] = plane_key[0]
    total[...] = jnp.full(total.shape, -1.0, jnp.float32)

    pl.semaphore_wait(barrier, (groups - 1) + 1 + 2 * (layers - 1))

    def start_column_keys(s):
        column_key_copy(s, 0).start()
        column_key_copy(s, 1).start()

    each_if(sends, lambda s: column_copy(s).start())
    each(groups, lambda s: plane_copy(s).start())
    pass_copy(0).start()
    each_if(sends, start_column_keys)
    each(groups, lambda s: plane_key_copy(s).start())
    column_key_copy(0, 1).start()

    def forward(s):
        column_copy(s).wait_recv()
        pass_copy(s).start()

    each_if(takes, forward)

    def plane_wait(s):
        plane_copy(s).wait_recv()
        plane_key_copy(s).wait_recv()

    each(groups, plane_wait)
    plane_cluster = jnp.concatenate([plane_key[s, 0:1] for s in range(groups)], axis=1)
    plane_rank = jnp.concatenate([plane_key[s, 1:2] for s in range(groups)], axis=1)

    def meet(s, both):
        rows = column[s].reshape(2 * items, width)
        others = plane[...].reshape(groups * lanes, width)
        scores = lax.dot_general(
            rows, others, (((1,), (1,)), ((), ())), preferred_element_type=jnp.float32
        )
        keys = [column_key[s, k].T[:items] for k in range(2)]
        cluster = jnp.concatenate([k[:, 0:1] for k in keys], axis=0)
        rank = jnp.concatenate([k[:, 1:2] for k in keys], axis=0)
        scores = jnp.where(cluster == plane_cluster, scores, -1.0)
        earlier = plane_rank < rank
        ahead = jnp.where(earlier, scores, -1.0)
        fold = ahead[:, :lanes]
        for b in range(1, groups):
            fold = jnp.maximum(fold, ahead[:, b * lanes:(b + 1) * lanes])
        for k in range(2):
            best = jnp.max(fold[k * items:(k + 1) * items].T, axis=0, keepdims=True)
            column_res[s, k, 0:1, :items] = best
        if both:
            behind = jnp.where(earlier, -1.0, scores)
            best = jnp.max(behind, axis=0, keepdims=True)
            total[0:1] = jnp.maximum(total[0:1], best)

    pass_copy(0).wait_recv()
    column_key_copy(0, 1).wait_recv()
    meet(0, False)
    column_res_copy(0, 1).start()

    def cross(s):
        pass_copy(s).wait_recv()
        column_key_copy(s, 0).wait_recv()
        column_key_copy(s, 1).wait_recv()
        meet(s, True)
        column_res_copy(s, 0).start()
        column_res_copy(s, 1).start()

    each_if(takes, cross)
    for s in range(groups):
        plane_res[s, 0:1] = total[0:1, s * lanes:(s + 1) * lanes]
    each(groups, lambda s: plane_res_copy(s).start())

    total[0:1, :items] = jnp.maximum(column_res[0, 0, 0:1, :items], plane_res[0, 0:1, :items])

    def take(got):
        total[0:1, :items] = jnp.maximum(total[0:1, :items], got[0:1, :items])

    column_res_copy(0, 1).wait_recv()
    take(column_got[0, 1])

    def take_column(s):
        for k in range(2):
            column_res_copy(s, k).wait_recv()
            take(column_got[s, k])

    def take_plane(s):
        plane_res_copy(s).wait_recv()
        take(plane_got[s])

    each_if(sends, take_column)
    each(groups, take_plane)
    out_ref[...] = total[0:1, :items].reshape(items)

    def sent_plane(s):
        plane_copy(s).wait_send()
        plane_key_copy(s).wait_send()
        plane_res_copy(s).wait_send()

    def sent_out(s):
        column_copy(s).wait_send()
        column_key_copy(s, 0).wait_send()
        column_key_copy(s, 1).wait_send()

    def sent_in(s):
        pass_copy(s).wait_send()
        column_res_copy(s, 0).wait_send()
        column_res_copy(s, 1).wait_send()

    each(groups, sent_plane)
    each_if(sends, sent_out)
    each_if(takes, sent_in)
    pass_copy(0).wait_send()
    column_key_copy(0, 1).wait_send()
    column_res_copy(0, 1).wait_send()


def per_device(embeds, cluster, priority):
    groups, layers = lax.axis_size("grp"), lax.axis_size("dev") // 2
    items, width = embeds.shape
    lanes = -(-items // LANES) * LANES
    dma = pltpu.SemaphoreType.DMA
    in_vmem = pl.BlockSpec(memory_space=pltpu.VMEM)
    return pl.pallas_call(
        functools.partial(kernel, groups, layers),
        out_shape=jax.ShapeDtypeStruct((items,), jnp.float32),
        in_specs=[in_vmem] * 3,
        out_specs=in_vmem,
        scratch_shapes=[
            pltpu.VMEM((groups, lanes, width), jnp.bfloat16),
            pltpu.VMEM((layers, 2, items, width), jnp.bfloat16),
            pltpu.VMEM((groups, 8, lanes), jnp.int32),
            pltpu.VMEM((layers, 2, 8, lanes), jnp.int32),
            pltpu.VMEM((groups, 8, lanes), jnp.float32),
            pltpu.VMEM((layers, 2, 8, lanes), jnp.float32),
            pltpu.VMEM((groups, 8, lanes), jnp.float32),
            pltpu.VMEM((layers, 2, 8, lanes), jnp.float32),
            pltpu.VMEM((8, groups * lanes), jnp.float32),
            dma((groups,)), dma((groups,)),
            dma((layers,)), dma((layers,)),
            dma((layers,)), dma((layers,)),
            dma((groups,)), dma((groups,)),
            dma((layers, 2)), dma((layers, 2)),
            dma((groups,)), dma((groups,)),
            dma((layers, 2)), dma((layers, 2)),
        ],
        compiler_params=pltpu.CompilerParams(
            collective_id=0, has_side_effects=True, vmem_limit_bytes=40 * 1024 * 1024
        ),
    )(embeds, cluster, priority)


def solution(mesh):
    in_specs = (P(("grp", "dev"), None), P(("grp", "dev")), P(("grp", "dev")))
    out_specs = P(("grp", "dev"))
    return jax.shard_map(
        per_device, mesh=mesh, in_specs=in_specs, out_specs=out_specs, check_vma=False
    )
```

```python
import functools

import jax
import jax.numpy as jnp
from jax import lax
from jax.experimental import pallas as pl
from jax.experimental.pallas import tpu as pltpu
from jax.sharding import PartitionSpec as P

MESH = pl.DeviceIdType.MESH
LANES = 128


def kernel(
    groups, layers, embeds_hbm, cluster_hbm, priority_hbm, out_ref,
    embeds_ref, cluster_ref, priority_ref,
    plane, column, plane_key, column_key, plane_res, column_res, plane_got, column_got, total,
    load_sem, plane_send, plane_recv, relay_send, relay_recv, pass_send, pass_recv,
    column_send, column_recv, plane_key_send, plane_key_recv, column_key_send, column_key_recv,
    plane_res_send, plane_res_recv, column_res_send, column_res_recv,
):
    items, width = embeds_ref.shape
    lanes = plane.shape[2]
    half = items // 2
    lows = 2 if groups % 2 == 0 else 1
    highs = groups // lows
    g, d = lax.axis_index("grp"), lax.axis_index("dev")
    z, c = d // 2, d % 2

    def at(group, layer, core):
        return {"grp": group, "dev": layer * 2 + core}

    def group_up(s):
        high, low = s // lows, s % lows
        return (g // lows + high) % highs * lows + (g % lows + low) % lows

    def group_down(s):
        high, low = s // lows, s % lows
        return (g // lows + highs - high) % highs * lows + (g % lows + lows - low) % lows

    def layer_up(s):
        return (z + s) % layers

    def layer_down(s):
        return (z + layers - s) % layers

    def core(k):
        return (c + k) % 2

    def sends(s):
        return (s % 2 == 0) & (z + s < layers) | (s % 2 == 1) & (z + s >= layers)

    def takes(s):
        return (s % 2 == 0) & (z >= s) | (s % 2 == 1) & (z < s)

    def remote(src, dst, send, recv, device):
        return pltpu.make_async_remote_copy(
            src_ref=src, dst_ref=dst, send_sem=send, recv_sem=recv,
            device_id=device, device_id_type=MESH,
        )

    def each_if(test, body):
        def step(s, carry):
            pl.when(test(s))(lambda: body(s))
            return carry
        lax.fori_loop(1, layers, step, 0)

    near = [s for s in range(1, groups) if s < lows or s % lows == 0]
    far = [s for s in range(1, groups) if s not in near]
    peers = [(s, k) for s in range(groups) for k in range(2) if (s, k) != (0, 0)]

    def plane_copy(s):
        return remote(plane.at[0, 0, pl.ds(0, items)], plane.at[s, 0, pl.ds(0, items)],
                      plane_send.at[s], plane_recv.at[s], at(group_up(s), z, c))

    def relay_copy(s, h):
        rows = pl.ds(h * half, half)
        low, high = s % lows, s - s % lows
        source, way = (low, high) if h == 0 else (high, low)
        return remote(plane.at[source, 0, rows], plane.at[s, 0, rows],
                      relay_send.at[s, h], relay_recv.at[s, h], at(group_up(way), z, c))

    def pass_copy(s):
        return remote(plane.at[s, 0, pl.ds(0, items)], plane.at[s, 1, pl.ds(0, items)],
                      pass_send.at[s], pass_recv.at[s], at(g, z, core(1)))

    def column_copy(s):
        return remote(column.at[0], column.at[s],
                      column_send.at[s], column_recv.at[s], at(g, layer_up(s), c))

    def plane_key_copy(s, k):
        return remote(plane_key.at[0, 0], plane_key.at[s, k],
                      plane_key_send.at[s, k], plane_key_recv.at[s, k], at(group_up(s), z, core(k)))

    def column_key_copy(s):
        return remote(column_key.at[0], column_key.at[s],
                      column_key_send.at[s], column_key_recv.at[s], at(g, layer_up(s), c))

    def plane_res_copy(s, k):
        return remote(plane_res.at[s, k], plane_got.at[s, k],
                      plane_res_send.at[s, k], plane_res_recv.at[s, k], at(group_down(s), z, core(k)))

    def column_res_copy(s):
        return remote(column_res.at[s], column_got.at[s],
                      column_res_send.at[s], column_res_recv.at[s], at(g, layer_down(s), c))

    loads = [
        pltpu.make_async_copy(src, dst, load_sem.at[i])
        for i, (src, dst) in enumerate(
            [(embeds_hbm, embeds_ref), (cluster_hbm, cluster_ref), (priority_hbm, priority_ref)]
        )
    ]
    for load in loads:
        load.start()

    barrier = pltpu.get_barrier_semaphore()

    def greet(device):
        pl.semaphore_signal(barrier, inc=1, device_id=device, device_id_type=MESH)

    lax.fori_loop(1, layers, lambda s, carry: (greet(at(g, layer_up(s), c)), carry)[1], 0)
    for s, k in peers:
        greet(at(group_up(s), z, core(k)))

    if lanes > items:
        for s in range(groups):
            for k in range(2):
                plane[s, k, items:] = jnp.zeros((lanes - items, width), jnp.bfloat16)
    plane_key[0, 0] = jnp.full((8, lanes), -1, jnp.int32)
    total[...] = jnp.full(total.shape, -1.0, jnp.float32)
    for load in loads:
        load.wait()
    values = embeds_ref[...].astype(jnp.float32)
    normed = (values * lax.rsqrt(jnp.sum(values * values, axis=1, keepdims=True) + 1e-06)).astype(
        jnp.bfloat16
    )
    plane[0, 0, :items] = normed
    column[0] = normed
    plane_key[0, 0, 0:1, :items] = cluster_ref[...].reshape(1, items)
    plane_key[0, 0, 1:2, :items] = priority_ref[...].reshape(1, items)
    column_key[0] = plane_key[0, 0]

    pl.semaphore_wait(barrier, len(peers) + layers - 1)

    each_if(sends, lambda s: column_copy(s).start())
    for s in near:
        plane_copy(s).start()
    pass_copy(0).start()
    each_if(sends, lambda s: column_key_copy(s).start())
    for s, k in peers:
        plane_key_copy(s, k).start()

    for s in near:
        plane_copy(s).wait_recv()
        for t in far:
            if s == t % lows:
                relay_copy(t, 0).start()
            if s == t - t % lows:
                relay_copy(t, 1).start()
        pass_copy(s).start()
    for s in far:
        relay_copy(s, 0).wait_recv()
        relay_copy(s, 1).wait_recv()
        pass_copy(s).start()
    for s, k in peers:
        plane_key_copy(s, k).wait_recv()
    every = [(s, k) for s in range(groups) for k in range(2)]
    plane_cluster = jnp.concatenate([plane_key[s, k, 0:1] for s, k in every], axis=1)
    plane_rank = jnp.concatenate([plane_key[s, k, 1:2] for s, k in every], axis=1)
    for s in range(groups):
        pass_copy(s).wait_recv()

    def meet(s, both):
        others = plane[...].reshape(groups * 2 * lanes, width)
        scores = lax.dot_general(
            column[s], others, (((1,), (1,)), ((), ())), preferred_element_type=jnp.float32
        )
        key = column_key[s].T[:items]
        cluster, rank = key[:, 0:1], key[:, 1:2]
        scores = jnp.where(cluster == plane_cluster, scores, -1.0)
        earlier = plane_rank < rank
        ahead = jnp.where(earlier, scores, -1.0)
        fold = ahead[:, :lanes]
        for b in range(1, len(every)):
            fold = jnp.maximum(fold, ahead[:, b * lanes:(b + 1) * lanes])
        column_res[s, 0:1, :items] = jnp.max(fold.T, axis=0, keepdims=True)
        if both:
            behind = jnp.where(earlier, -1.0, scores)
            best = jnp.max(behind, axis=0, keepdims=True)
            total[0:1] = jnp.maximum(total[0:1], best)

    meet(0, False)

    def cross(s):
        column_copy(s).wait_recv()
        column_key_copy(s).wait_recv()
        meet(s, True)
        column_res_copy(s).start()

    each_if(takes, cross)
    for b, (s, k) in enumerate(every):
        plane_res[s, k, 0:1] = total[0:1, b * lanes:(b + 1) * lanes]
    for s, k in peers:
        plane_res_copy(s, k).start()

    total[0:1, :items] = jnp.maximum(column_res[0, 0:1, :items], plane_res[0, 0, 0:1, :items])

    def take_column(s):
        column_res_copy(s).wait_recv()
        total[0:1, :items] = jnp.maximum(total[0:1, :items], column_got[s, 0:1, :items])

    each_if(sends, take_column)
    for s, k in peers:
        plane_res_copy(s, k).wait_recv()
    best = total[0:1, :items]
    for s, k in peers:
        best = jnp.maximum(best, plane_got[s, k, 0:1, :items])
    out_ref[...] = best.reshape(items)

    for s in near:
        plane_copy(s).wait_send()
    for s in far:
        relay_copy(s, 0).wait_send()
        relay_copy(s, 1).wait_send()
    for s in range(groups):
        pass_copy(s).wait_send()
    for s, k in peers:
        plane_key_copy(s, k).wait_send()
        plane_res_copy(s, k).wait_send()

    def sent_out(s):
        column_copy(s).wait_send()
        column_key_copy(s).wait_send()

    each_if(sends, sent_out)
    each_if(takes, lambda s: column_res_copy(s).wait_send())


def per_device(embeds, cluster, priority):
    groups, layers = lax.axis_size("grp"), lax.axis_size("dev") // 2
    items, width = embeds.shape
    lanes = -(-items // LANES) * LANES
    dma = pltpu.SemaphoreType.DMA
    return pl.pallas_call(
        functools.partial(kernel, groups, layers),
        out_shape=jax.ShapeDtypeStruct((items,), jnp.float32),
        in_specs=[pl.BlockSpec(memory_space=pltpu.HBM)] * 3,
        out_specs=pl.BlockSpec(memory_space=pltpu.VMEM),
        scratch_shapes=[
            pltpu.VMEM((items, width), jnp.bfloat16),
            pltpu.VMEM((items,), jnp.int32),
            pltpu.VMEM((items,), jnp.int32),
            pltpu.VMEM((groups, 2, lanes, width), jnp.bfloat16),
            pltpu.VMEM((layers, items, width), jnp.bfloat16),
            pltpu.VMEM((groups, 2, 8, lanes), jnp.int32),
            pltpu.VMEM((layers, 8, lanes), jnp.int32),
            pltpu.VMEM((groups, 2, 8, lanes), jnp.float32),
            pltpu.VMEM((layers, 8, lanes), jnp.float32),
            pltpu.VMEM((groups, 2, 8, lanes), jnp.float32),
            pltpu.VMEM((layers, 8, lanes), jnp.float32),
            pltpu.VMEM((8, groups * 2 * lanes), jnp.float32),
            dma((3,)),
            dma((groups,)), dma((groups,)),
            dma((groups, 2)), dma((groups, 2)),
            dma((groups,)), dma((groups,)),
            dma((layers,)), dma((layers,)),
            dma((groups, 2)), dma((groups, 2)),
            dma((layers,)), dma((layers,)),
            dma((groups, 2)), dma((groups, 2)),
            dma((layers,)), dma((layers,)),
        ],
        compiler_params=pltpu.CompilerParams(
            collective_id=0, has_side_effects=True, vmem_limit_bytes=40 * 1024 * 1024
        ),
    )(embeds, cluster, priority)


def solution(mesh):
    in_specs = (P(("grp", "dev"), None), P(("grp", "dev")), P(("grp", "dev")))
    out_specs = P(("grp", "dev"))
    return jax.shard_map(
        per_device, mesh=mesh, in_specs=in_specs, out_specs=out_specs, check_vma=False
    )
```

```python
import functools

import jax
import jax.numpy as jnp
from jax import lax
from jax.experimental import pallas as pl
from jax.experimental.pallas import tpu as pltpu
from jax.sharding import PartitionSpec as P

MESH = pl.DeviceIdType.MESH
LANES = 128


def kernel(
    groups, layers, embeds_hbm, cluster_hbm, priority_hbm, out_ref,
    embeds_ref, cluster_ref, priority_ref,
    plane, column, plane_key, column_key, plane_res, column_res, plane_got, column_got, total,
    load_sem, plane_send, plane_recv, relay_send, relay_recv, pass_send, pass_recv,
    column_send, column_recv, plane_key_send, plane_key_recv, column_key_send, column_key_recv,
    plane_res_send, plane_res_recv, column_res_send, column_res_recv,
):
    items, width = embeds_ref.shape
    lanes = plane.shape[2]
    half = items // 2
    lows = 2 if groups % 2 == 0 else 1
    highs = groups // lows
    g, d = lax.axis_index("grp"), lax.axis_index("dev")
    z, c = d // 2, d % 2

    def at(group, layer, core):
        return {"grp": group, "dev": layer * 2 + core}

    def group_up(s):
        high, low = s // lows, s % lows
        return (g // lows + high) % highs * lows + (g % lows + low) % lows

    def group_down(s):
        high, low = s // lows, s % lows
        return (g // lows + highs - high) % highs * lows + (g % lows + lows - low) % lows

    def layer_up(s):
        return (z + s) % layers

    def layer_down(s):
        return (z + layers - s) % layers

    def core(k):
        return (c + k) % 2

    def sends(s):
        return (s % 2 == 0) & (z + s < layers) | (s % 2 == 1) & (z + s >= layers)

    def takes(s):
        return (s % 2 == 0) & (z >= s) | (s % 2 == 1) & (z < s)

    def remote(src, dst, send, recv, device):
        return pltpu.make_async_remote_copy(
            src_ref=src, dst_ref=dst, send_sem=send, recv_sem=recv,
            device_id=device, device_id_type=MESH,
        )

    def each_if(test, body):
        def step(s, carry):
            pl.when(test(s))(lambda: body(s))
            return carry
        lax.fori_loop(1, layers, step, 0)

    near = [s for s in range(1, groups) if s < lows or s % lows == 0]
    far = [s for s in range(1, groups) if s not in near]
    peers = [(s, k) for s in range(groups) for k in range(2) if (s, k) != (0, 0)]

    def plane_copy(s):
        return remote(plane.at[0, 0, pl.ds(0, items)], plane.at[s, 0, pl.ds(0, items)],
                      plane_send.at[s], plane_recv.at[s], at(group_up(s), z, c))

    def relay_copy(s, h):
        rows = pl.ds(h * half, half)
        low, high = s % lows, s - s % lows
        source, way = (low, high) if h == 0 else (high, low)
        return remote(plane.at[source, 0, rows], plane.at[s, 0, rows],
                      relay_send.at[s, h], relay_recv.at[s, h], at(group_up(way), z, c))

    def pass_copy(s):
        return remote(plane.at[s, 0, pl.ds(0, items)], plane.at[s, 1, pl.ds(0, items)],
                      pass_send.at[s], pass_recv.at[s], at(g, z, core(1)))

    def column_copy(s):
        return remote(column.at[0], column.at[s],
                      column_send.at[s], column_recv.at[s], at(g, layer_up(s), c))

    def plane_key_copy(s, k):
        return remote(plane_key.at[0, 0], plane_key.at[s, k],
                      plane_key_send.at[s, k], plane_key_recv.at[s, k], at(group_up(s), z, core(k)))

    def column_key_copy(s):
        return remote(column_key.at[0], column_key.at[s],
                      column_key_send.at[s], column_key_recv.at[s], at(g, layer_up(s), c))

    def plane_res_copy(s, k):
        return remote(plane_res.at[s, k], plane_got.at[s, k],
                      plane_res_send.at[s, k], plane_res_recv.at[s, k], at(group_down(s), z, core(k)))

    def column_res_copy(s):
        return remote(column_res.at[s], column_got.at[s],
                      column_res_send.at[s], column_res_recv.at[s], at(g, layer_down(s), c))

    loads = [
        pltpu.make_async_copy(src, dst, load_sem.at[i])
        for i, (src, dst) in enumerate(
            [(embeds_hbm, embeds_ref), (cluster_hbm, cluster_ref), (priority_hbm, priority_ref)]
        )
    ]
    for load in loads:
        load.start()

    barrier = pltpu.get_barrier_semaphore()

    def greet(device):
        pl.semaphore_signal(barrier, inc=1, device_id=device, device_id_type=MESH)

    lax.fori_loop(1, layers, lambda s, carry: (greet(at(g, layer_up(s), c)), carry)[1], 0)
    for s, k in peers:
        greet(at(group_up(s), z, core(k)))

    if lanes > items:
        for s in range(groups):
            for k in range(2):
                plane[s, k, items:] = jnp.zeros((lanes - items, width), jnp.bfloat16)
    plane_key[0, 0] = jnp.full((8, lanes), -1, jnp.int32)
    total[...] = jnp.full(total.shape, -1.0, jnp.float32)
    for load in loads:
        load.wait()
    values = embeds_ref[...].astype(jnp.float32)
    normed = (values * lax.rsqrt(jnp.sum(values * values, axis=1, keepdims=True) + 1e-06)).astype(
        jnp.bfloat16
    )
    plane[0, 0, :items] = normed
    column[0] = normed
    plane_key[0, 0, 0:1, :items] = cluster_ref[...].reshape(1, items)
    plane_key[0, 0, 1:2, :items] = priority_ref[...].reshape(1, items)
    column_key[0] = plane_key[0, 0]

    pl.semaphore_wait(barrier, len(peers) + layers - 1)

    each_if(sends, lambda s: column_copy(s).start())
    for s in near:
        plane_copy(s).start()
    pass_copy(0).start()
    each_if(sends, lambda s: column_key_copy(s).start())
    for s, k in peers:
        plane_key_copy(s, k).start()

    for s in near:
        plane_copy(s).wait_recv()
        for t in far:
            if s == t % lows:
                relay_copy(t, 0).start()
            if s == t - t % lows:
                relay_copy(t, 1).start()
        pass_copy(s).start()
    for s in far:
        relay_copy(s, 0).wait_recv()
        relay_copy(s, 1).wait_recv()
        pass_copy(s).start()
    for s, k in peers:
        plane_key_copy(s, k).wait_recv()
    every = [(s, k) for s in range(groups) for k in range(2)]
    plane_cluster = jnp.concatenate([plane_key[s, k, 0:1] for s, k in every], axis=1)
    plane_rank = jnp.concatenate([plane_key[s, k, 1:2] for s, k in every], axis=1)
    for s in range(groups):
        pass_copy(s).wait_recv()

    def meet(s, both):
        others = plane[...].reshape(groups * 2 * lanes, width)
        scores = lax.dot_general(
            column[s], others, (((1,), (1,)), ((), ())), preferred_element_type=jnp.float32
        )
        key = column_key[s].T[:items]
        cluster, rank = key[:, 0:1], key[:, 1:2]
        scores = jnp.where(cluster == plane_cluster, scores, -1.0)
        earlier = plane_rank < rank
        ahead = jnp.where(earlier, scores, -1.0)
        fold = ahead[:, :lanes]
        for b in range(1, len(every)):
            fold = jnp.maximum(fold, ahead[:, b * lanes:(b + 1) * lanes])
        column_res[s, 0:1, :items] = jnp.max(fold.T, axis=0, keepdims=True)
        if both:
            behind = jnp.where(earlier, -1.0, scores)
            best = jnp.max(behind, axis=0, keepdims=True)
            total[0:1] = jnp.maximum(total[0:1], best)

    meet(0, False)

    def cross(s):
        column_copy(s).wait_recv()
        column_key_copy(s).wait_recv()
        meet(s, True)
        column_res_copy(s).start()

    each_if(takes, cross)
    for b, (s, k) in enumerate(every):
        plane_res[s, k, 0:1] = total[0:1, b * lanes:(b + 1) * lanes]
    for s, k in peers:
        plane_res_copy(s, k).start()

    total[0:1, :items] = jnp.maximum(column_res[0, 0:1, :items], plane_res[0, 0, 0:1, :items])

    def take_column(s):
        column_res_copy(s).wait_recv()
        total[0:1, :items] = jnp.maximum(total[0:1, :items], column_got[s, 0:1, :items])

    each_if(sends, take_column)
    for s, k in peers:
        plane_res_copy(s, k).wait_recv()
    best = total[0:1, :items]
    for s, k in peers:
        best = jnp.maximum(best, plane_got[s, k, 0:1, :items])
    out_ref[...] = best.reshape(items)

    for s in near:
        plane_copy(s).wait_send()
    for s in far:
        relay_copy(s, 0).wait_send()
        relay_copy(s, 1).wait_send()
    for s in range(groups):
        pass_copy(s).wait_send()
    for s, k in peers:
        plane_key_copy(s, k).wait_send()
        plane_res_copy(s, k).wait_send()

    def sent_out(s):
        column_copy(s).wait_send()
        column_key_copy(s).wait_send()

    each_if(sends, sent_out)
    each_if(takes, lambda s: column_res_copy(s).wait_send())


def per_device(embeds, cluster, priority):
    groups, layers = lax.axis_size("grp"), lax.axis_size("dev") // 2
    items, width = embeds.shape
    lanes = -(-items // LANES) * LANES
    dma = pltpu.SemaphoreType.DMA
    return pl.pallas_call(
        functools.partial(kernel, groups, layers),
        out_shape=jax.ShapeDtypeStruct((items,), jnp.float32),
        in_specs=[pl.BlockSpec(memory_space=pltpu.HBM)] * 3,
        out_specs=pl.BlockSpec(memory_space=pltpu.VMEM),
        scratch_shapes=[
            pltpu.VMEM((items, width), jnp.bfloat16),
            pltpu.VMEM((items,), jnp.int32),
            pltpu.VMEM((items,), jnp.int32),
            pltpu.VMEM((groups, 2, lanes, width), jnp.bfloat16),
            pltpu.VMEM((layers, items, width), jnp.bfloat16),
            pltpu.VMEM((groups, 2, 8, lanes), jnp.int32),
            pltpu.VMEM((layers, 8, lanes), jnp.int32),
            pltpu.VMEM((groups, 2, 8, lanes), jnp.float32),
            pltpu.VMEM((layers, 8, lanes), jnp.float32),
            pltpu.VMEM((groups, 2, 8, lanes), jnp.float32),
            pltpu.VMEM((layers, 8, lanes), jnp.float32),
            pltpu.VMEM((8, groups * 2 * lanes), jnp.float32),
            dma((3,)),
            dma((groups,)), dma((groups,)),
            dma((groups, 2)), dma((groups, 2)),
            dma((groups,)), dma((groups,)),
            dma((layers,)), dma((layers,)),
            dma((groups, 2)), dma((groups, 2)),
            dma((layers,)), dma((layers,)),
            dma((groups, 2)), dma((groups, 2)),
            dma((layers,)), dma((layers,)),
        ],
        compiler_params=pltpu.CompilerParams(
            collective_id=0, has_side_effects=True, vmem_limit_bytes=64 * 1024 * 1024
        ),
    )(embeds, cluster, priority)


def solution(mesh):
    in_specs = (P(("grp", "dev"), None), P(("grp", "dev")), P(("grp", "dev")))
    out_specs = P(("grp", "dev"))
    return jax.shard_map(
        per_device, mesh=mesh, in_specs=in_specs, out_specs=out_specs, check_vma=False
    )
```

```python
import functools

import jax
import jax.numpy as jnp
from jax import lax
from jax.experimental import pallas as pl
from jax.experimental.pallas import tpu as pltpu
from jax.sharding import PartitionSpec as P

MESH = pl.DeviceIdType.MESH
LANES = 128


def kernel(
    groups, layers, embeds_hbm, cluster_hbm, priority_hbm, out_ref,
    embeds_ref, cluster_ref, priority_ref,
    plane, column, plane_key, column_key, plane_res, column_res, plane_got, column_got, total,
    load_sem, plane_send, plane_recv, relay_send, relay_recv, pass_send, pass_recv,
    column_send, column_recv, plane_key_send, plane_key_recv, column_key_send, column_key_recv,
    plane_res_send, plane_res_recv, column_res_send, column_res_recv,
):
    items, width = embeds_ref.shape
    lanes = plane.shape[2]
    half = items // 2
    lows = 2 if groups % 2 == 0 else 1
    highs = groups // lows
    g, d = lax.axis_index("grp"), lax.axis_index("dev")
    z, c = d // 2, d % 2

    def at(group, layer, core):
        return {"grp": group, "dev": layer * 2 + core}

    def group_up(s):
        high, low = s // lows, s % lows
        return (g // lows + high) % highs * lows + (g % lows + low) % lows

    def group_down(s):
        high, low = s // lows, s % lows
        return (g // lows + highs - high) % highs * lows + (g % lows + lows - low) % lows

    def layer_up(s):
        return (z + s) % layers

    def layer_down(s):
        return (z + layers - s) % layers

    def core(k):
        return (c + k) % 2

    def sends(s):
        return (s % 2 == 0) & (z + s < layers) | (s % 2 == 1) & (z + s >= layers)

    def takes(s):
        return (s % 2 == 0) & (z >= s) | (s % 2 == 1) & (z < s)

    def remote(src, dst, send, recv, device):
        return pltpu.make_async_remote_copy(
            src_ref=src, dst_ref=dst, send_sem=send, recv_sem=recv,
            device_id=device, device_id_type=MESH,
        )

    def each_if(test, body):
        def step(s, carry):
            pl.when(test(s))(lambda: body(s))
            return carry
        lax.fori_loop(1, layers, step, 0)

    near = [s for s in range(1, groups) if s < lows or s % lows == 0]
    far = [s for s in range(1, groups) if s not in near]
    peers = [(s, k) for s in range(groups) for k in range(2) if (s, k) != (0, 0)]

    def plane_copy(s):
        return remote(plane.at[0, 0, pl.ds(0, items)], plane.at[s, 0, pl.ds(0, items)],
                      plane_send.at[s], plane_recv.at[s], at(group_up(s), z, c))

    def relay_copy(s, h):
        rows = pl.ds(h * half, half)
        low, high = s % lows, s - s % lows
        source, way = (low, high) if h == 0 else (high, low)
        return remote(plane.at[source, 0, rows], plane.at[s, 0, rows],
                      relay_send.at[s, h], relay_recv.at[s, h], at(group_up(way), z, c))

    def pass_copy(s):
        return remote(plane.at[s, 0, pl.ds(0, items)], plane.at[s, 1, pl.ds(0, items)],
                      pass_send.at[s], pass_recv.at[s], at(g, z, core(1)))

    def column_copy(s):
        return remote(column.at[0], column.at[s],
                      column_send.at[s], column_recv.at[s], at(g, layer_up(s), c))

    def plane_key_copy(s, k):
        return remote(plane_key.at[0, 0], plane_key.at[s, k],
                      plane_key_send.at[s, k], plane_key_recv.at[s, k], at(group_up(s), z, core(k)))

    def column_key_copy(s):
        return remote(column_key.at[0], column_key.at[s],
                      column_key_send.at[s], column_key_recv.at[s], at(g, layer_up(s), c))

    def plane_res_copy(s, k):
        return remote(plane_res.at[s, k], plane_got.at[s, k],
                      plane_res_send.at[s, k], plane_res_recv.at[s, k], at(group_down(s), z, core(k)))

    def column_res_copy(s):
        return remote(column_res.at[s], column_got.at[s],
                      column_res_send.at[s], column_res_recv.at[s], at(g, layer_down(s), c))

    loads = [
        pltpu.make_async_copy(src, dst, load_sem.at[i])
        for i, (src, dst) in enumerate(
            [(embeds_hbm, embeds_ref), (cluster_hbm, cluster_ref), (priority_hbm, priority_ref)]
        )
    ]
    for load in loads:
        load.start()

    barrier = pltpu.get_barrier_semaphore()

    def greet(device):
        pl.semaphore_signal(barrier, inc=1, device_id=device, device_id_type=MESH)

    lax.fori_loop(1, layers, lambda s, carry: (greet(at(g, layer_up(s), c)), carry)[1], 0)
    for s, k in peers:
        greet(at(group_up(s), z, core(k)))

    if lanes > items:
        for s in range(groups):
            for k in range(2):
                plane[s, k, items:] = jnp.zeros((lanes - items, width), jnp.bfloat16)
    plane_key[0, 0] = jnp.full((8, lanes), -1, jnp.int32)
    total[...] = jnp.full(total.shape, -1.0, jnp.float32)
    for load in loads:
        load.wait()
    values = embeds_ref[...].astype(jnp.float32)
    normed = (values * lax.rsqrt(jnp.sum(values * values, axis=1, keepdims=True) + 1e-06)).astype(
        jnp.bfloat16
    )
    plane[0, 0, :items] = normed
    column[0] = normed
    plane_key[0, 0, 0:1, :items] = cluster_ref[...].reshape(1, items)
    plane_key[0, 0, 1:2, :items] = priority_ref[...].reshape(1, items)
    column_key[0] = plane_key[0, 0]

    pl.semaphore_wait(barrier, len(peers) + layers - 1)

    each_if(sends, lambda s: column_copy(s).start())
    for s in near:
        plane_copy(s).start()
    pass_copy(0).start()
    each_if(sends, lambda s: column_key_copy(s).start())
    for s, k in peers:
        plane_key_copy(s, k).start()

    for s in near:
        plane_copy(s).wait_recv()
        for t in far:
            if s == t % lows:
                relay_copy(t, 0).start()
            if s == t - t % lows:
                relay_copy(t, 1).start()
        pass_copy(s).start()
    for s in far:
        relay_copy(s, 0).wait_recv()
        relay_copy(s, 1).wait_recv()
        pass_copy(s).start()
    for s, k in peers:
        plane_key_copy(s, k).wait_recv()
    every = [(s, k) for s in range(groups) for k in range(2)]
    plane_cluster = jnp.concatenate([plane_key[s, k, 0:1] for s, k in every], axis=1)
    plane_rank = jnp.concatenate([plane_key[s, k, 1:2] for s, k in every], axis=1)
    for s in range(groups):
        pass_copy(s).wait_recv()

    def meet(s, both):
        others = plane[...].reshape(groups * 2 * lanes, width)
        scores = lax.dot_general(
            column[s], others, (((1,), (1,)), ((), ())), preferred_element_type=jnp.float32
        )
        key = column_key[s].T[:items]
        cluster, rank = key[:, 0:1], key[:, 1:2]
        scores = jnp.where(cluster == plane_cluster, scores, -1.0)
        earlier = plane_rank < rank
        ahead = jnp.where(earlier, scores, -1.0)
        fold = ahead[:, :lanes]
        for b in range(1, len(every)):
            fold = jnp.maximum(fold, ahead[:, b * lanes:(b + 1) * lanes])
        column_res[s, 0:1, :items] = jnp.max(fold.T, axis=0, keepdims=True)
        if both:
            behind = jnp.where(earlier, -1.0, scores)
            best = jnp.max(behind, axis=0, keepdims=True)
            total[0:1] = jnp.maximum(total[0:1], best)

    meet(0, False)

    def cross(s):
        column_copy(s).wait_recv()
        column_key_copy(s).wait_recv()
        meet(s, True)
        column_res_copy(s).start()

    each_if(takes, cross)
    for b, (s, k) in enumerate(every):
        plane_res[s, k, 0:1] = total[0:1, b * lanes:(b + 1) * lanes]
    for s, k in peers:
        plane_res_copy(s, k).start()

    total[0:1, :items] = jnp.maximum(column_res[0, 0:1, :items], plane_res[0, 0, 0:1, :items])

    def take_column(s):
        column_res_copy(s).wait_recv()
        total[0:1, :items] = jnp.maximum(total[0:1, :items], column_got[s, 0:1, :items])

    each_if(sends, take_column)
    for s, k in peers:
        plane_res_copy(s, k).wait_recv()
    best = total[0:1, :items]
    for s, k in peers:
        best = jnp.maximum(best, plane_got[s, k, 0:1, :items])
    out_ref[...] = best.reshape(items)

    for s in near:
        plane_copy(s).wait_send()
    for s in far:
        relay_copy(s, 0).wait_send()
        relay_copy(s, 1).wait_send()
    for s in range(groups):
        pass_copy(s).wait_send()
    for s, k in peers:
        plane_key_copy(s, k).wait_send()
        plane_res_copy(s, k).wait_send()

    def sent_out(s):
        column_copy(s).wait_send()
        column_key_copy(s).wait_send()

    each_if(sends, sent_out)
    each_if(takes, lambda s: column_res_copy(s).wait_send())


def per_device(embeds, cluster, priority):
    groups, layers = lax.axis_size("grp"), lax.axis_size("dev") // 2
    items, width = embeds.shape
    lanes = -(-items // LANES) * LANES
    dma = pltpu.SemaphoreType.DMA
    return pl.pallas_call(
        functools.partial(kernel, groups, layers),
        out_shape=jax.ShapeDtypeStruct((items,), jnp.float32),
        in_specs=[pl.BlockSpec(memory_space=pltpu.HBM)] * 3,
        out_specs=pl.BlockSpec(memory_space=pltpu.VMEM),
        scratch_shapes=[
            pltpu.VMEM((items, width), jnp.bfloat16),
            pltpu.VMEM((items,), jnp.int32),
            pltpu.VMEM((items,), jnp.int32),
            pltpu.VMEM((groups, 2, lanes, width), jnp.bfloat16),
            pltpu.VMEM((layers, items, width), jnp.bfloat16),
            pltpu.VMEM((groups, 2, 8, lanes), jnp.int32),
            pltpu.VMEM((layers, 8, lanes), jnp.int32),
            pltpu.VMEM((groups, 2, 8, lanes), jnp.float32),
            pltpu.VMEM((layers, 8, lanes), jnp.float32),
            pltpu.VMEM((groups, 2, 8, lanes), jnp.float32),
            pltpu.VMEM((layers, 8, lanes), jnp.float32),
            pltpu.VMEM((8, groups * 2 * lanes), jnp.float32),
            dma((3,)),
            dma((groups,)), dma((groups,)),
            dma((groups, 2)), dma((groups, 2)),
            dma((groups,)), dma((groups,)),
            dma((layers,)), dma((layers,)),
            dma((groups, 2)), dma((groups, 2)),
            dma((layers,)), dma((layers,)),
            dma((groups, 2)), dma((groups, 2)),
            dma((layers,)), dma((layers,)),
        ],
        compiler_params=pltpu.CompilerParams(
            collective_id=0, has_side_effects=True, vmem_limit_bytes=40 * 1024 * 1024
        ),
    )(*[pltpu.with_memory_space_constraint(x, pltpu.HBM) for x in (embeds, cluster, priority)])


def solution(mesh):
    in_specs = (P(("grp", "dev"), None), P(("grp", "dev")), P(("grp", "dev")))
    out_specs = P(("grp", "dev"))
    return jax.shard_map(
        per_device, mesh=mesh, in_specs=in_specs, out_specs=out_specs, check_vma=False
    )
```

```python
import functools

import jax
import jax.numpy as jnp
from jax import lax
from jax.experimental import pallas as pl
from jax.experimental.pallas import tpu as pltpu
from jax.sharding import PartitionSpec as P

MESH = pl.DeviceIdType.MESH
LANES = 128


def kernel(
    groups, layers, embeds_hbm, cluster_hbm, priority_hbm, out_ref,
    embeds_ref, cluster_ref, priority_ref,
    plane, column, plane_key, column_key, plane_res, column_res, plane_got, column_got, total,
    partial, own_fold, load_sem, plane_send, plane_recv, relay_send, relay_recv, pass_send, pass_recv,
    column_send, column_recv, plane_key_send, plane_key_recv, column_key_send, column_key_recv,
    plane_res_send, plane_res_recv, column_res_send, column_res_recv,
):
    items, width = embeds_ref.shape
    lanes = plane.shape[2]
    slots = column_recv.shape[0]
    half, depth = items // 2, width // 2
    lows = 2 if groups % 2 == 0 else 1
    highs = groups // lows
    batch = 2 if slots % 2 == 0 else 1
    batches = slots // batch
    g, d = lax.axis_index("grp"), lax.axis_index("dev")
    z, c = d // 2, d % 2

    def at(group, layer, core):
        return {"grp": group, "dev": layer * 2 + core}

    def group_up(s):
        high, low = s // lows, s % lows
        return (g // lows + high) % highs * lows + (g % lows + low) % lows

    def group_down(s):
        high, low = s // lows, s % lows
        return (g // lows + highs - high) % highs * lows + (g % lows + lows - low) % lows

    def layer_up(s):
        return (z + s) % layers

    def core(k):
        return (c + k) % 2

    def sends(s):
        return (s % 2 == 0) & (z + s < layers) | (s % 2 == 1) & (z + s >= layers)

    def first_odd(layer):
        return layer + 1 + layer % 2

    def slot_of(s):
        to = layer_up(s)
        return (1 - s % 2) * (s // 2 - 1) + (s % 2) * (to // 2 + (s - first_odd(to)) // 2)

    def offset_of(j):
        return jnp.where(j < z // 2, 2 * (j + 1), first_odd(z) + 2 * (j - z // 2))

    def filled(j):
        return j < z // 2 + (layers + 1 - first_odd(z)) // 2

    def remote(src, dst, send, recv, device):
        return pltpu.make_async_remote_copy(
            src_ref=src, dst_ref=dst, send_sem=send, recv_sem=recv,
            device_id=device, device_id_type=MESH,
        )

    def each(start, count, body):
        if count <= 4:
            for i in range(start, count):
                body(i)
        else:
            lax.fori_loop(start, count, lambda i, carry: (body(i), carry)[1], 0)

    def each_if(start, count, test, body):
        each(start, count, lambda i: pl.when(test(i))(lambda: body(i)))

    near = [s for s in range(1, groups) if s < lows or s % lows == 0]
    far = [s for s in range(1, groups) if s not in near]
    every = [(s, k) for s in range(groups) for k in range(2)]
    peers = every[1:]

    def rows_of(h):
        return pl.ds(h * half, half)

    def plane_copy(s, h):
        return remote(plane.at[0, 0, rows_of(h)], plane.at[s, 0, rows_of(h)],
                      plane_send.at[s, h], plane_recv.at[s, h], at(group_up(s), z, c))

    def relay_copy(s, h):
        low, high = s % lows, s - s % lows
        source, way = (low, high) if h == 0 else (high, low)
        return remote(plane.at[source, 0, rows_of(h)], plane.at[s, 0, rows_of(h)],
                      relay_send.at[s, h], relay_recv.at[s, h], at(group_up(way), z, c))

    def pass_copy(s):
        return remote(plane.at[s, 0, pl.ds(0, items)], plane.at[s, 1, pl.ds(0, items)],
                      pass_send.at[s], pass_recv.at[s], at(g, z, core(1)))

    def column_copy(s, j, h):
        columns = pl.ds(h * depth, depth)
        return remote(plane.at[0, 0, pl.ds(0, items), columns], column.at[j, pl.ds(0, items), columns],
                      column_send.at[s, h], column_recv.at[j, h], at(g, layer_up(s), c))

    def plane_key_copy(s, k):
        return remote(plane_key.at[0, 0], plane_key.at[s, k],
                      plane_key_send.at[s, k], plane_key_recv.at[s, k], at(group_up(s), z, core(k)))

    def column_key_copy(s, j):
        return remote(plane_key.at[0, 0], column_key.at[j],
                      column_key_send.at[s], column_key_recv.at[j], at(g, layer_up(s), c))

    def plane_res_copy(s, k):
        return remote(plane_res.at[s, k], plane_got.at[s, k],
                      plane_res_send.at[s, k], plane_res_recv.at[s, k], at(group_down(s), z, core(k)))

    def column_res_copy(j, s):
        return remote(column_res.at[j], column_got.at[s],
                      column_res_send.at[j], column_res_recv.at[s], at(g, (z + layers - s) % layers, c))

    loads = [
        pltpu.make_async_copy(src, dst, load_sem.at[i])
        for i, (src, dst) in enumerate(
            [(embeds_hbm, embeds_ref), (cluster_hbm, cluster_ref), (priority_hbm, priority_ref)]
        )
    ]
    for load in loads:
        load.start()

    barrier = pltpu.get_barrier_semaphore()

    def greet(device):
        pl.semaphore_signal(barrier, inc=1, device_id=device, device_id_type=MESH)

    column_key[...] = jnp.full(column_key.shape, -2, jnp.int32)
    each(1, layers, lambda s: greet(at(g, layer_up(s), c)))
    for s, k in peers:
        greet(at(group_up(s), z, core(k)))

    if lanes > items:
        for s, k in every:
            plane[s, k, items:] = jnp.zeros((lanes - items, width), jnp.bfloat16)
    plane_key[0, 0] = jnp.full((8, lanes), -1, jnp.int32)
    total[...] = jnp.full(total.shape, -1.0, jnp.float32)
    own_fold[...] = jnp.full(own_fold.shape, -1.0, jnp.float32)
    for load in loads:
        load.wait()
    values = embeds_ref[...].astype(jnp.float32)
    normed = (values * lax.rsqrt(jnp.sum(values * values, axis=1, keepdims=True) + 1e-06)).astype(
        jnp.bfloat16
    )
    plane[0, 0, :items] = normed
    plane_key[0, 0, 0:1, :items] = cluster_ref[...].reshape(1, items)
    plane_key[0, 0, 1:2, :items] = priority_ref[...].reshape(1, items)

    pl.semaphore_wait(barrier, len(peers) + layers - 1)

    def first_half(s):
        return 0 if s < lows else 1

    for i in range(2):
        each_if(1, layers, sends, lambda s: column_copy(s, slot_of(s), i).start())
        for s in near:
            plane_copy(s, first_half(s) if i == 0 else 1 - first_half(s)).start()
    pass_copy(0).start()
    for s, k in peers:
        plane_key_copy(s, k).start()
    each_if(1, layers, sends, lambda s: column_key_copy(s, slot_of(s)).start())

    for s in near:
        plane_copy(s, first_half(s)).wait_recv()
        for t in far:
            if s == t % lows:
                relay_copy(t, 0).start()
            if s == t - t % lows:
                relay_copy(t, 1).start()

    def plane_keys(s):
        return (jnp.concatenate([plane_key[s, k, i:i + 1] for k in range(2)], axis=1) for i in range(2))

    def column_keys(key):
        key = key.T[:items]
        return key[:, 0:1], key[:, 1:2]

    def folded(scores):
        return jnp.maximum(scores[:, :lanes], scores[:, lanes:])

    def product(rows, others):
        return lax.dot_general(
            rows, others, (((1,), (1,)), ((), ())), preferred_element_type=jnp.float32
        )

    def others_of(s):
        return plane[s].reshape(2 * lanes, width)

    def meet_own(s):
        pass_copy(s).wait_recv()
        for k in range(2):
            if (s, k) != (0, 0):
                plane_key_copy(s, k).wait_recv()
        scores = product(plane[0, 0, :items], others_of(s))
        cluster, rank = column_keys(plane_key[0, 0])
        plane_cluster, plane_rank = plane_keys(s)
        chosen = (cluster == plane_cluster) & (plane_rank < rank)
        own_fold[...] = jnp.maximum(own_fold[...], folded(jnp.where(chosen, scores, -1.0)))

    def block(j, h):
        return column[pl.ds(j * batch, batch), :, h * depth:(h + 1) * depth].reshape(batch * items, depth)

    def arrive(j, h):
        def wait(i):
            column_copy(1, i, h).wait_recv()
            if h == 0:
                column_key_copy(1, i).wait_recv()
        for i in range(batch):
            pl.when(filled(j * batch + i))(functools.partial(wait, j * batch + i))

    def meet_first(j, s):
        partial[s] = product(block(j, 0), others_of(s)[:, :depth])

    def meet_second(j, last):
        arrive(j, 1)
        keys = [column_keys(column_key[j * batch + i]) for i in range(batch)]
        cluster = jnp.concatenate([key[0] for key in keys], axis=0)
        rank = jnp.concatenate([key[1] for key in keys], axis=0)
        fold = jnp.full((batch * items, lanes), -1.0, jnp.float32)
        for s in reversed(range(groups)):
            scores = partial[s] + product(block(j, 1), others_of(s)[:, depth:])
            plane_cluster, plane_rank = plane_keys(s)
            scores = jnp.where(cluster == plane_cluster, scores, -1.0)
            earlier = plane_rank < rank
            fold = jnp.maximum(fold, folded(jnp.where(earlier, scores, -1.0)))
            best = jnp.max(jnp.where(earlier, -1.0, scores), axis=0, keepdims=True)
            for k in range(2):
                here = slice((2 * s + k) * lanes, (2 * s + k + 1) * lanes)
                total[0:1, here] = jnp.maximum(total[0:1, here], best[:, k * lanes:(k + 1) * lanes])
            if last:
                send_plane(s)
        for i in range(batch):
            rows = fold[i * items:(i + 1) * items]
            column_res[j * batch + i, 0:1, :items] = jnp.max(rows.T, axis=0, keepdims=True)

            def send(slot):
                column_res_copy(slot, offset_of(slot)).start()
            pl.when(filled(j * batch + i))(functools.partial(send, j * batch + i))

    def send_plane(s):
        for k in range(2):
            plane_res[s, k, 0:1] = total[0:1, (2 * s + k) * lanes:(2 * s + k + 1) * lanes]
            if (s, k) != (0, 0):
                plane_res_copy(s, k).start()

    meet_own(0)
    for s in near:
        plane_copy(s, 1 - first_half(s)).wait_recv()
        pass_copy(s).start()
    for s in far:
        relay_copy(s, 0).wait_recv()
        relay_copy(s, 1).wait_recv()
        pass_copy(s).start()
    for s in near:
        meet_own(s)
    if batches == 1:
        arrive(0, 0)
        for s in [0] + near:
            meet_first(0, s)
    for s in far:
        meet_own(s)
    if batches == 1:
        for s in far:
            meet_first(0, s)
        meet_second(0, True)
    else:
        def step(j):
            arrive(j, 0)
            for s in range(groups):
                meet_first(j, s)
            meet_second(j, False)
        each(0, batches, step)
        for s in range(groups):
            send_plane(s)

    best = jnp.max(own_fold[...].T, axis=0, keepdims=True)
    best = jnp.maximum(best, plane_res[0, 0, 0:1, :items])
    for s, k in peers:
        plane_res_copy(s, k).wait_recv()
        best = jnp.maximum(best, plane_got[s, k, 0:1, :items])
    total[0:1, :items] = best

    def take_column(s):
        column_res_copy(0, s).wait_recv()
        total[0:1, :items] = jnp.maximum(total[0:1, :items], column_got[s, 0:1, :items])

    each_if(1, layers, sends, take_column)
    out_ref[...] = total[0:1, :items].reshape(items)

    for s in near:
        for h in range(2):
            plane_copy(s, h).wait_send()
    for s in far:
        for h in range(2):
            relay_copy(s, h).wait_send()
    for s in range(groups):
        pass_copy(s).wait_send()
    for s, k in peers:
        plane_key_copy(s, k).wait_send()
        plane_res_copy(s, k).wait_send()

    def sent_out(s):
        for h in range(2):
            column_copy(s, 0, h).wait_send()
        column_key_copy(s, 0).wait_send()

    each_if(1, layers, sends, sent_out)
    each_if(0, slots, filled, lambda j: column_res_copy(j, 1).wait_send())


def per_device(embeds, cluster, priority):
    groups, layers = lax.axis_size("grp"), lax.axis_size("dev") // 2
    slots = layers // 2
    items, width = embeds.shape
    lanes = -(-items // LANES) * LANES
    batch = 2 if slots % 2 == 0 else 1
    dma = pltpu.SemaphoreType.DMA
    some = max(slots, 1)
    return pl.pallas_call(
        functools.partial(kernel, groups, layers),
        out_shape=jax.ShapeDtypeStruct((items,), jnp.float32),
        in_specs=[pl.BlockSpec(memory_space=pltpu.HBM)] * 3,
        out_specs=pl.BlockSpec(memory_space=pltpu.VMEM),
        scratch_shapes=[
            pltpu.VMEM((items, width), jnp.bfloat16),
            pltpu.VMEM((items,), jnp.int32),
            pltpu.VMEM((items,), jnp.int32),
            pltpu.VMEM((groups, 2, lanes, width), jnp.bfloat16),
            pltpu.VMEM((some, items, width), jnp.bfloat16),
            pltpu.VMEM((groups, 2, 8, lanes), jnp.int32),
            pltpu.VMEM((some, 8, lanes), jnp.int32),
            pltpu.VMEM((groups, 2, 8, lanes), jnp.float32),
            pltpu.VMEM((some, 8, lanes), jnp.float32),
            pltpu.VMEM((groups, 2, 8, lanes), jnp.float32),
            pltpu.VMEM((layers, 8, lanes), jnp.float32),
            pltpu.VMEM((8, groups * 2 * lanes), jnp.float32),
            pltpu.VMEM((groups, batch * items, 2 * lanes), jnp.float32),
            pltpu.VMEM((items, lanes), jnp.float32),
            dma((3,)),
            dma((groups, 2)), dma((groups, 2)),
            dma((groups, 2)), dma((groups, 2)),
            dma((groups,)), dma((groups,)),
            dma((layers, 2)), dma((some, 2)),
            dma((groups, 2)), dma((groups, 2)),
            dma((layers,)), dma((some,)),
            dma((groups, 2)), dma((groups, 2)),
            dma((some,)), dma((layers,)),
        ],
        compiler_params=pltpu.CompilerParams(
            collective_id=0, has_side_effects=True, vmem_limit_bytes=40 * 1024 * 1024
        ),
    )(*[pltpu.with_memory_space_constraint(x, pltpu.HBM) for x in (embeds, cluster, priority)])


def solution(mesh):
    in_specs = (P(("grp", "dev"), None), P(("grp", "dev")), P(("grp", "dev")))
    out_specs = P(("grp", "dev"))
    return jax.shard_map(
        per_device, mesh=mesh, in_specs=in_specs, out_specs=out_specs, check_vma=False
    )
```

```python
import functools

import jax
import jax.numpy as jnp
from jax import lax
from jax.experimental import pallas as pl
from jax.experimental.pallas import tpu as pltpu
from jax.sharding import PartitionSpec as P

MESH = pl.DeviceIdType.MESH
LANES = 128


def kernel(
    groups, layers, embeds_hbm, cluster_hbm, priority_hbm, out_ref,
    embeds_ref, cluster_ref, priority_ref,
    plane, normal, column, plane_key, column_key, plane_res, column_res, plane_got, column_got, total,
    partial, own_best, load_sem, plane_send, plane_recv, relay_send, relay_recv, pass_send, pass_recv,
    column_send, column_recv, plane_key_send, plane_key_recv, column_key_send, column_key_recv,
    plane_res_send, plane_res_recv, column_res_send, column_res_recv,
):
    items, width = embeds_ref.shape
    lanes = plane_key.shape[3]
    slots = column_recv.shape[0]
    half = items // 2
    cut = width // 4 * 3
    parts = [(0, cut), (cut, width - cut)]
    lows = 2 if groups % 2 == 0 else 1
    highs = groups // lows
    batch = 2 if slots % 2 == 0 else 1
    batches = slots // batch
    g, d = lax.axis_index("grp"), lax.axis_index("dev")
    z, c = d // 2, d % 2

    def at(group, layer, core):
        return {"grp": group, "dev": layer * 2 + core}

    def group_up(s):
        high, low = s // lows, s % lows
        return (g // lows + high) % highs * lows + (g % lows + low) % lows

    def group_down(s):
        high, low = s // lows, s % lows
        return (g // lows + highs - high) % highs * lows + (g % lows + lows - low) % lows

    def layer_up(s):
        return (z + s) % layers

    def core(k):
        return (c + k) % 2

    def sends(s):
        return (s % 2 == 0) & (z + s < layers) | (s % 2 == 1) & (z + s >= layers)

    def first_odd(layer):
        return layer + 1 + layer % 2

    def slot_of(s):
        to = layer_up(s)
        return (1 - s % 2) * (s // 2 - 1) + (s % 2) * (to // 2 + (s - first_odd(to)) // 2)

    def offset_of(j):
        return jnp.where(j < z // 2, 2 * (j + 1), first_odd(z) + 2 * (j - z // 2))

    def filled(j):
        return j < z // 2 + (layers + 1 - first_odd(z)) // 2

    def remote(src, dst, send, recv, device):
        return pltpu.make_async_remote_copy(
            src_ref=src, dst_ref=dst, send_sem=send, recv_sem=recv,
            device_id=device, device_id_type=MESH,
        )

    def each(start, count, body):
        if count <= 4:
            for i in range(start, count):
                body(i)
        else:
            lax.fori_loop(start, count, lambda i, carry: (body(i), carry)[1], 0)

    def each_if(start, count, test, body):
        each(start, count, lambda i: pl.when(test(i))(lambda: body(i)))

    near = [s for s in range(1, groups) if s < lows or s % lows == 0]
    far = [s for s in range(1, groups) if s not in near]
    every = [(s, k) for s in range(groups) for k in range(2)]
    peers = every[1:]

    def rows_of(h):
        return pl.ds(h * half, half)

    def plane_copy(s, h):
        return remote(embeds_hbm.at[rows_of(h)], plane.at[s, 0, rows_of(h)],
                      plane_send.at[s, h], plane_recv.at[s, h], at(group_up(s), z, c))

    def relay_copy(s, h):
        low, high = s % lows, s - s % lows
        source, way = (low, high) if h == 0 else (high, low)
        return remote(plane.at[source, 0, rows_of(h)], plane.at[s, 0, rows_of(h)],
                      relay_send.at[s, h], relay_recv.at[s, h], at(group_up(way), z, c))

    def pass_copy(s):
        return remote(plane.at[s, 0] if s else embeds_hbm, plane.at[s, 1],
                      pass_send.at[s], pass_recv.at[s], at(g, z, core(1)))

    def column_copy(s, j, h):
        columns = pl.ds(*parts[h])
        return remote(embeds_hbm.at[:, columns], column.at[j, :, columns],
                      column_send.at[s, h], column_recv.at[j, h], at(g, layer_up(s), c))

    def plane_key_copy(s, k):
        return remote(plane_key.at[0, 0], plane_key.at[s, k],
                      plane_key_send.at[s, k], plane_key_recv.at[s, k], at(group_up(s), z, core(k)))

    def column_key_copy(s, j):
        return remote(plane_key.at[0, 0], column_key.at[j],
                      column_key_send.at[s], column_key_recv.at[j], at(g, layer_up(s), c))

    def plane_res_copy(s, k):
        return remote(plane_res.at[s, k], plane_got.at[s, k],
                      plane_res_send.at[s, k], plane_res_recv.at[s, k], at(group_down(s), z, core(k)))

    def column_res_copy(j, s):
        return remote(column_res.at[j], column_got.at[s],
                      column_res_send.at[j], column_res_recv.at[s], at(g, (z + layers - s) % layers, c))

    loads = [
        pltpu.make_async_copy(src, dst, load_sem.at[i])
        for i, (src, dst) in enumerate(
            [(embeds_hbm, embeds_ref), (cluster_hbm, cluster_ref), (priority_hbm, priority_ref)]
        )
    ]
    for load in loads:
        load.start()

    barrier = pltpu.get_barrier_semaphore()

    def greet(device):
        pl.semaphore_signal(barrier, inc=1, device_id=device, device_id_type=MESH)

    column_key[...] = jnp.full(column_key.shape, -2.0, jnp.float32)
    each(1, layers, lambda s: greet(at(g, layer_up(s), c)))
    for s, k in peers:
        greet(at(group_up(s), z, core(k)))

    pl.semaphore_wait(barrier, len(peers) + layers - 1)

    def first_half(s):
        return 0 if s < lows else 1

    for i in range(2):
        each_if(1, layers, sends, lambda s: column_copy(s, slot_of(s), i).start())
        for s in near:
            plane_copy(s, first_half(s) if i == 0 else 1 - first_half(s)).start()
    pass_copy(0).start()

    total[...] = jnp.full(total.shape, -1.0, jnp.float32)
    plane_key[0, 0] = jnp.full((8, lanes), -1.0, jnp.float32)
    for load in loads:
        load.wait()
    values = embeds_ref[...].astype(jnp.float32)
    scale = lax.rsqrt(jnp.sum(values * values, axis=1, keepdims=True) + 1e-06)
    normal[0, 0] = (values * scale).astype(jnp.bfloat16)
    plane_key[0, 0, 0:1, :items] = cluster_ref[...].reshape(1, items).astype(jnp.float32)
    plane_key[0, 0, 1:2, :items] = priority_ref[...].reshape(1, items).astype(jnp.float32)
    plane_key[0, 0, 2:3, :items] = jnp.broadcast_to(scale, (items, LANES)).T[0:1]
    for s, k in peers:
        plane_key_copy(s, k).start()
    each_if(1, layers, sends, lambda s: column_key_copy(s, slot_of(s)).start())

    for s in near:
        plane_copy(s, first_half(s)).wait_recv()
        for t in far:
            if s == t % lows:
                relay_copy(t, 0).start()
            if s == t - t % lows:
                relay_copy(t, 1).start()

    def column_keys(key):
        key = key.T[:items]
        return key[:, 0:1], key[:, 1:2], key[:, 2:3]

    def lane_keys(blocks, i):
        return jnp.concatenate([plane_key[s, k, i:i + 1, :items] for s, k in blocks], axis=1)

    def product(rows, others):
        return lax.dot_general(
            rows, others, (((1,), (1,)), ((), ())), preferred_element_type=jnp.float32
        )

    def scaled(rows, scale):
        return (rows.astype(jnp.float32) * scale).astype(jnp.bfloat16)

    def meet_own(s):
        pass_copy(s).wait_recv()
        for k in range(2):
            if (s, k) != (0, 0):
                plane_key_copy(s, k).wait_recv()
                normal[s, k] = scaled(plane[s, k], column_keys(plane_key[s, k])[2])
        blocks = [(s, 0), (s, 1)]
        scores = product(normal[0, 0], normal[s].reshape(2 * items, width))
        cluster, rank, _ = column_keys(plane_key[0, 0])
        chosen = (cluster == lane_keys(blocks, 0)) & (lane_keys(blocks, 1) < rank)
        best = jnp.max(jnp.where(chosen, scores, -1.0), axis=1, keepdims=True)
        own_best[...] = best if s == 0 else jnp.maximum(own_best[...], best)

    def arrive(j, h):
        def wait(i):
            column_copy(1, i, h).wait_recv()
            if h == 0:
                column_key_copy(1, i).wait_recv()
        for i in range(batch):
            pl.when(filled(j * batch + i))(functools.partial(wait, j * batch + i))

    def batch_keys(j):
        keys = [column_keys(column_key[j * batch + i]) for i in range(batch)]
        return [jnp.concatenate([key[r] for key in keys], axis=0) for r in range(3)]

    def part_product(j, h, scale):
        start, size = parts[h]
        rows = column[pl.ds(j * batch, batch), :, start:start + size].reshape(batch * items, size)
        others = normal[:, :, :, start:start + size].reshape(len(every) * items, size)
        return product(scaled(rows, scale), others)

    def meet_column(j):
        arrive(j, 0)
        cluster, rank, scale = batch_keys(j)
        partial[...] = part_product(j, 0, scale)
        plane_cluster, plane_rank = lane_keys(every, 0), lane_keys(every, 1)
        arrive(j, 1)
        scores = partial[...] + part_product(j, 1, scale)
        scores = jnp.where(cluster == plane_cluster, scores, -1.0)
        earlier = plane_rank < rank
        best = jnp.max(jnp.where(earlier, -1.0, scores), axis=0, keepdims=True)
        total[0:1] = jnp.maximum(total[0:1], best)
        if batches == 1:
            send_plane()
        ahead = jnp.where(earlier, scores, -1.0)
        fold = ahead[:, :LANES]
        for start in range(LANES, ahead.shape[1], LANES):
            fold = jnp.maximum(fold, ahead[:, start:start + LANES])
        for i in range(batch):
            rows = fold[i * items:(i + 1) * items]
            column_res[j * batch + i, 0:1, :items] = jnp.max(rows.T, axis=0, keepdims=True)

            def send(slot):
                column_res_copy(slot, offset_of(slot)).start()
            pl.when(filled(j * batch + i))(functools.partial(send, j * batch + i))

    def send_plane():
        for b, (s, k) in enumerate(every):
            plane_res[s, k, 0:1, :items] = total[0:1, b * items:(b + 1) * items]
        for s, k in reversed(peers):
            plane_res_copy(s, k).start()

    meet_own(0)
    for s in near:
        plane_copy(s, 1 - first_half(s)).wait_recv()
        pass_copy(s).start()
    for s in far:
        relay_copy(s, 0).wait_recv()
        relay_copy(s, 1).wait_recv()
        pass_copy(s).start()
    for s in near + far:
        meet_own(s)
    if batches == 1:
        meet_column(0)
    else:
        each(0, batches, meet_column)
        send_plane()

    best = jnp.broadcast_to(own_best[...], (items, LANES)).T[0:1]
    best = jnp.maximum(best, plane_res[0, 0, 0:1, :items])
    for s, k in peers:
        plane_res_copy(s, k).wait_recv()
        best = jnp.maximum(best, plane_got[s, k, 0:1, :items])
    total[0:1, :items] = best

    def take_column(s):
        column_res_copy(0, s).wait_recv()
        total[0:1, :items] = jnp.maximum(total[0:1, :items], column_got[s, 0:1, :items])

    each_if(1, layers, sends, take_column)
    out_ref[...] = total[0:1, :items].reshape(items)

    for s in near:
        for h in range(2):
            plane_copy(s, h).wait_send()
    for s in far:
        for h in range(2):
            relay_copy(s, h).wait_send()
    for s in range(groups):
        pass_copy(s).wait_send()
    for s, k in peers:
        plane_key_copy(s, k).wait_send()
        plane_res_copy(s, k).wait_send()

    def sent_out(s):
        for h in range(2):
            column_copy(s, 0, h).wait_send()
        column_key_copy(s, 0).wait_send()

    each_if(1, layers, sends, sent_out)
    each_if(0, slots, filled, lambda j: column_res_copy(j, 1).wait_send())


def per_device(embeds, cluster, priority):
    groups, layers = lax.axis_size("grp"), lax.axis_size("dev") // 2
    slots = layers // 2
    items, width = embeds.shape
    lanes = -(-items // LANES) * LANES
    batch = 2 if slots % 2 == 0 else 1
    dma = pltpu.SemaphoreType.DMA
    some = max(slots, 1)
    return pl.pallas_call(
        functools.partial(kernel, groups, layers),
        out_shape=jax.ShapeDtypeStruct((items,), jnp.float32),
        in_specs=[pl.BlockSpec(memory_space=pltpu.HBM)] * 3,
        out_specs=pl.BlockSpec(memory_space=pltpu.VMEM),
        scratch_shapes=[
            pltpu.VMEM((items, width), jnp.bfloat16),
            pltpu.VMEM((items,), jnp.int32),
            pltpu.VMEM((items,), jnp.int32),
            pltpu.VMEM((groups, 2, items, width), jnp.bfloat16),
            pltpu.VMEM((groups, 2, items, width), jnp.bfloat16),
            pltpu.VMEM((some, items, width), jnp.bfloat16),
            pltpu.VMEM((groups, 2, 8, lanes), jnp.float32),
            pltpu.VMEM((some, 8, lanes), jnp.float32),
            pltpu.VMEM((groups, 2, 8, lanes), jnp.float32),
            pltpu.VMEM((some, 8, lanes), jnp.float32),
            pltpu.VMEM((groups, 2, 8, lanes), jnp.float32),
            pltpu.VMEM((layers, 8, lanes), jnp.float32),
            pltpu.VMEM((8, groups * 2 * items), jnp.float32),
            pltpu.VMEM((batch * items, groups * 2 * items), jnp.float32),
            pltpu.VMEM((items, 1), jnp.float32),
            dma((3,)),
            dma((groups, 2)), dma((groups, 2)),
            dma((groups, 2)), dma((groups, 2)),
            dma((groups,)), dma((groups,)),
            dma((layers, 2)), dma((some, 2)),
            dma((groups, 2)), dma((groups, 2)),
            dma((layers,)), dma((some,)),
            dma((groups, 2)), dma((groups, 2)),
            dma((some,)), dma((layers,)),
        ],
        compiler_params=pltpu.CompilerParams(
            collective_id=0, has_side_effects=True, vmem_limit_bytes=40 * 1024 * 1024
        ),
    )(*[pltpu.with_memory_space_constraint(x, pltpu.HBM) for x in (embeds, cluster, priority)])


def solution(mesh):
    in_specs = (P(("grp", "dev"), None), P(("grp", "dev")), P(("grp", "dev")))
    out_specs = P(("grp", "dev"))
    return jax.shard_map(
        per_device, mesh=mesh, in_specs=in_specs, out_specs=out_specs, check_vma=False
    )
```

```python
import functools

import jax
import jax.numpy as jnp
from jax import lax
from jax.experimental import pallas as pl
from jax.experimental.pallas import tpu as pltpu
from jax.sharding import PartitionSpec as P

MESH = pl.DeviceIdType.MESH
LANES = 128


def batch_of(slots):
    return 0 if slots == 0 else 2 if slots % 2 == 0 else 1


def kernel(
    groups, layers, embeds_hbm, cluster_hbm, priority_hbm, out_ref,
    embeds_ref, cluster_ref, priority_ref,
    plane, normal, column, plane_key, column_key, plane_res, column_res, plane_got, column_got, total,
    own_res, partial, load_sem, plane_send, plane_recv, relay_send, relay_recv, pass_send, pass_recv,
    column_send, column_recv, plane_key_send, plane_key_recv, column_key_send, column_key_recv,
    plane_res_send, plane_res_recv, column_res_send, column_res_recv,
):
    items, width = embeds_ref.shape
    lanes = plane_key.shape[3]
    slots = layers // 2
    half = items // 2
    cut = width // 4 * 3
    parts = [(0, cut), (cut, width - cut)]
    lows = 2 if groups % 2 == 0 else 1
    highs = groups // lows
    batch = batch_of(slots)
    batches = slots // batch if slots else 1
    g, d = lax.axis_index("grp"), lax.axis_index("dev")
    z, c = d // 2, d % 2

    def at(group, layer, core):
        return {"grp": group, "dev": layer * 2 + core}

    def group_up(s):
        high, low = s // lows, s % lows
        return (g // lows + high) % highs * lows + (g % lows + low) % lows

    def group_down(s):
        high, low = s // lows, s % lows
        return (g // lows + highs - high) % highs * lows + (g % lows + lows - low) % lows

    def layer_up(s):
        return (z + s) % layers

    def core(k):
        return (c + k) % 2

    def sends(s):
        return (s % 2 == 0) & (z + s < layers) | (s % 2 == 1) & (z + s >= layers)

    def first_odd(layer):
        return layer + 1 + layer % 2

    def slot_of(s):
        to = layer_up(s)
        return (1 - s % 2) * (s // 2 - 1) + (s % 2) * (to // 2 + (s - first_odd(to)) // 2)

    def offset_of(j):
        return jnp.where(j < z // 2, 2 * (j + 1), first_odd(z) + 2 * (j - z // 2))

    def filled(j):
        return j < z // 2 + (layers + 1 - first_odd(z)) // 2

    def remote(src, dst, send, recv, device):
        return pltpu.make_async_remote_copy(
            src_ref=src, dst_ref=dst, send_sem=send, recv_sem=recv,
            device_id=device, device_id_type=MESH,
        )

    def each(start, count, body):
        if count <= 4:
            for i in range(start, count):
                body(i)
        else:
            lax.fori_loop(start, count, lambda i, carry: (body(i), carry)[1], 0)

    def each_if(start, count, test, body):
        each(start, count, lambda i: pl.when(test(i))(lambda: body(i)))

    near = [s for s in range(1, groups) if s < lows or s % lows == 0]
    far = [s for s in range(1, groups) if s not in near]
    every = [(s, k) for s in range(groups) for k in range(2)]
    peers = every[1:]

    def rows_of(h):
        return pl.ds(h * half, half)

    def plane_copy(s, h):
        return remote(embeds_hbm.at[rows_of(h)], plane.at[s, 0, rows_of(h)],
                      plane_send.at[s, h], plane_recv.at[s, h], at(group_up(s), z, c))

    def relay_copy(s, h):
        low, high = s % lows, s - s % lows
        source, way = (low, high) if h == 0 else (high, low)
        return remote(plane.at[source, 0, rows_of(h)], plane.at[s, 0, rows_of(h)],
                      relay_send.at[s, h], relay_recv.at[s, h], at(group_up(way), z, c))

    def pass_copy(s):
        return remote(plane.at[s, 0] if s else embeds_hbm, plane.at[s, 1],
                      pass_send.at[s], pass_recv.at[s], at(g, z, core(1)))

    def column_copy(s, j, h):
        columns = pl.ds(*parts[h])
        return remote(embeds_hbm.at[:, columns], column.at[j, :, columns],
                      column_send.at[s, h], column_recv.at[j, h], at(g, layer_up(s), c))

    def plane_key_copy(s, k):
        return remote(plane_key.at[0, 0], plane_key.at[s, k],
                      plane_key_send.at[s, k], plane_key_recv.at[s, k], at(group_up(s), z, core(k)))

    def column_key_copy(s, j):
        return remote(plane_key.at[0, 0], column_key.at[j],
                      column_key_send.at[s], column_key_recv.at[j], at(g, layer_up(s), c))

    def plane_res_copy(s, k):
        return remote(plane_res.at[s, k], plane_got.at[s, k],
                      plane_res_send.at[s, k], plane_res_recv.at[s, k], at(group_down(s), z, core(k)))

    def column_res_copy(j, s):
        return remote(column_res.at[j], column_got.at[s],
                      column_res_send.at[j], column_res_recv.at[s], at(g, (z + layers - s) % layers, c))

    loads = [
        pltpu.make_async_copy(src, dst, load_sem.at[i])
        for i, (src, dst) in enumerate(
            [(embeds_hbm, embeds_ref), (cluster_hbm, cluster_ref), (priority_hbm, priority_ref)]
        )
    ]
    for load in loads:
        load.start()

    barrier = pltpu.get_barrier_semaphore()

    def greet(device):
        pl.semaphore_signal(barrier, inc=1, device_id=device, device_id_type=MESH)

    column_key[...] = jnp.full(column_key.shape, -2.0, jnp.float32)
    each(1, layers, lambda s: greet(at(g, layer_up(s), c)))
    for s, k in peers:
        greet(at(group_up(s), z, core(k)))

    pl.semaphore_wait(barrier, len(peers) + layers - 1)

    def first_half(s):
        return 0 if s < lows else 1

    for i in range(2):
        each_if(1, layers, sends, lambda s: column_copy(s, slot_of(s), i).start())
        for s in near:
            plane_copy(s, first_half(s) if i == 0 else 1 - first_half(s)).start()
    pass_copy(0).start()

    total[...] = jnp.full(total.shape, -1.0, jnp.float32)
    plane_key[0, 0] = jnp.full((8, lanes), -1.0, jnp.float32)
    for load in loads:
        load.wait()
    values = embeds_ref[...].astype(jnp.float32)
    scale = lax.rsqrt(jnp.sum(values * values, axis=1, keepdims=True) + 1e-06)
    normal[0, 0] = (values * scale).astype(jnp.bfloat16)
    plane_key[0, 0, 0:1, :items] = cluster_ref[...].reshape(1, items).astype(jnp.float32)
    plane_key[0, 0, 1:2, :items] = priority_ref[...].reshape(1, items).astype(jnp.float32)
    plane_key[0, 0, 2:3, :items] = jnp.broadcast_to(scale, (items, LANES)).T[0:1]
    for s, k in peers:
        plane_key_copy(s, k).start()
    each_if(1, layers, sends, lambda s: column_key_copy(s, slot_of(s)).start())

    for s in near:
        plane_copy(s, first_half(s)).wait_recv()
        for t in far:
            if s == t % lows:
                relay_copy(t, 0).start()
            if s == t - t % lows:
                relay_copy(t, 1).start()

    def column_keys(key):
        key = key.T[:items]
        return key[:, 0:1], key[:, 1:2], key[:, 2:3]

    def lane_keys(blocks, i):
        return jnp.concatenate([plane_key[s, k, i:i + 1, :items] for s, k in blocks], axis=1)

    def product(rows, others):
        return lax.dot_general(
            rows, others, (((1,), (1,)), ((), ())), preferred_element_type=jnp.float32
        )

    def scaled(rows, scale):
        return (rows.astype(jnp.float32) * scale).astype(jnp.bfloat16)

    def scale_plane(s, k):
        normal[s, k] = scaled(plane[s, k], column_keys(plane_key[s, k])[2])

    def arrive(j, h):
        def wait(i):
            column_copy(1, i, h).wait_recv()
            if h == 0:
                column_key_copy(1, i).wait_recv()
        for i in range(batch):
            pl.when(filled(j * batch + i))(functools.partial(wait, j * batch + i))

    def part_product(j, h, scales):
        start, size = parts[h]
        here = slice(start, start + size)
        rows = [normal[0, 0, :, here]]
        rows += [scaled(column[j * batch + i, :, here], scales[i]) for i in range(batch)]
        return product(jnp.concatenate(rows, axis=0), normal[:, :, :, here].reshape(len(every) * items, size))

    def meet(j):
        arrive(j, 0)
        keys = [column_keys(plane_key[0, 0])] + [column_keys(column_key[j * batch + i]) for i in range(batch)]
        scales = [key[2] for key in keys[1:]]
        partial[...] = part_product(j, 0, scales)
        cluster, rank = (jnp.concatenate([key[i] for key in keys], axis=0) for i in range(2))
        plane_cluster, plane_rank = lane_keys(every, 0), lane_keys(every, 1)
        arrive(j, 1)
        scores = partial[...] + part_product(j, 1, scales)
        scores = jnp.where(cluster == plane_cluster, scores, -1.0)
        earlier = plane_rank < rank
        if batch:
            behind = jnp.where(earlier[items:], -1.0, scores[items:])
            total[0:1] = jnp.maximum(total[0:1], jnp.max(behind, axis=0, keepdims=True))
        if batches == 1:
            send_plane()
        ahead = jnp.where(earlier, scores, -1.0)
        fold = ahead[:, :LANES]
        for start in range(LANES, ahead.shape[1], LANES):
            fold = jnp.maximum(fold, ahead[:, start:start + LANES])

        def best_of(i):
            return jnp.max(fold[i * items:(i + 1) * items].T, axis=0, keepdims=True)

        for i in range(batch):
            column_res[j * batch + i, 0:1, :items] = best_of(1 + i)

            def send(slot):
                column_res_copy(slot, offset_of(slot)).start()
            pl.when(filled(j * batch + i))(functools.partial(send, j * batch + i))
        own_res[0:1, :items] = best_of(0)

    def send_plane():
        for b, (s, k) in enumerate(every):
            plane_res[s, k, 0:1, :items] = total[0:1, b * items:(b + 1) * items]
        for s, k in reversed(peers):
            plane_res_copy(s, k).start()

    pass_copy(0).wait_recv()
    for s, k in peers:
        plane_key_copy(s, k).wait_recv()
    scale_plane(0, 1)
    for s in near:
        plane_copy(s, 1 - first_half(s)).wait_recv()
        pass_copy(s).start()
        scale_plane(s, 0)
    for s in near:
        pass_copy(s).wait_recv()
        scale_plane(s, 1)
    for s in far:
        relay_copy(s, 0).wait_recv()
        relay_copy(s, 1).wait_recv()
        pass_copy(s).start()
        scale_plane(s, 0)
    for s in far:
        pass_copy(s).wait_recv()
        scale_plane(s, 1)
    if batches == 1:
        meet(0)
    else:
        each(0, batches, meet)
        send_plane()

    best = own_res[0:1, :items]
    best = jnp.maximum(best, plane_res[0, 0, 0:1, :items])
    for s, k in peers:
        plane_res_copy(s, k).wait_recv()
        best = jnp.maximum(best, plane_got[s, k, 0:1, :items])
    total[0:1, :items] = best

    def take_column(s):
        column_res_copy(0, s).wait_recv()
        total[0:1, :items] = jnp.maximum(total[0:1, :items], column_got[s, 0:1, :items])

    each_if(1, layers, sends, take_column)
    out_ref[...] = total[0:1, :items].reshape(items)

    for s in near:
        for h in range(2):
            plane_copy(s, h).wait_send()
    for s in far:
        for h in range(2):
            relay_copy(s, h).wait_send()
    for s in range(groups):
        pass_copy(s).wait_send()
    for s, k in peers:
        plane_key_copy(s, k).wait_send()
        plane_res_copy(s, k).wait_send()

    def sent_out(s):
        for h in range(2):
            column_copy(s, 0, h).wait_send()
        column_key_copy(s, 0).wait_send()

    each_if(1, layers, sends, sent_out)
    each_if(0, slots, filled, lambda j: column_res_copy(j, 1).wait_send())


def per_device(embeds, cluster, priority):
    groups, layers = lax.axis_size("grp"), lax.axis_size("dev") // 2
    slots = layers // 2
    items, width = embeds.shape
    lanes = -(-items // LANES) * LANES
    batch = batch_of(slots)
    dma = pltpu.SemaphoreType.DMA
    some = max(slots, 1)
    return pl.pallas_call(
        functools.partial(kernel, groups, layers),
        out_shape=jax.ShapeDtypeStruct((items,), jnp.float32),
        in_specs=[pl.BlockSpec(memory_space=pltpu.HBM)] * 3,
        out_specs=pl.BlockSpec(memory_space=pltpu.VMEM),
        scratch_shapes=[
            pltpu.VMEM((items, width), jnp.bfloat16),
            pltpu.VMEM((items,), jnp.int32),
            pltpu.VMEM((items,), jnp.int32),
            pltpu.VMEM((groups, 2, items, width), jnp.bfloat16),
            pltpu.VMEM((groups, 2, items, width), jnp.bfloat16),
            pltpu.VMEM((some, items, width), jnp.bfloat16),
            pltpu.VMEM((groups, 2, 8, lanes), jnp.float32),
            pltpu.VMEM((some, 8, lanes), jnp.float32),
            pltpu.VMEM((groups, 2, 8, lanes), jnp.float32),
            pltpu.VMEM((some, 8, lanes), jnp.float32),
            pltpu.VMEM((groups, 2, 8, lanes), jnp.float32),
            pltpu.VMEM((layers, 8, lanes), jnp.float32),
            pltpu.VMEM((8, groups * 2 * items), jnp.float32),
            pltpu.VMEM((8, lanes), jnp.float32),
            pltpu.VMEM(((1 + batch) * items, groups * 2 * items), jnp.float32),
            dma((3,)),
            dma((groups, 2)), dma((groups, 2)),
            dma((groups, 2)), dma((groups, 2)),
            dma((groups,)), dma((groups,)),
            dma((layers, 2)), dma((some, 2)),
            dma((groups, 2)), dma((groups, 2)),
            dma((layers,)), dma((some,)),
            dma((groups, 2)), dma((groups, 2)),
            dma((some,)), dma((layers,)),
        ],
        compiler_params=pltpu.CompilerParams(
            collective_id=0, has_side_effects=True, vmem_limit_bytes=40 * 1024 * 1024
        ),
    )(*[pltpu.with_memory_space_constraint(x, pltpu.HBM) for x in (embeds, cluster, priority)])


def solution(mesh):
    in_specs = (P(("grp", "dev"), None), P(("grp", "dev")), P(("grp", "dev")))
    out_specs = P(("grp", "dev"))
    return jax.shard_map(
        per_device, mesh=mesh, in_specs=in_specs, out_specs=out_specs, check_vma=False
    )
```

```python
import functools

import jax
import jax.numpy as jnp
from jax import lax
from jax.experimental import pallas as pl
from jax.experimental.pallas import tpu as pltpu
from jax.sharding import PartitionSpec as P

MESH = pl.DeviceIdType.MESH
LANES = 128


def batch_of(slots):
    return 0 if slots == 0 else 2 if slots % 2 == 0 else 1


def kernel(
    groups, layers, embeds_hbm, cluster_hbm, priority_hbm, out_ref,
    embeds_ref, cluster_ref, priority_ref,
    plane, normal, column, plane_key, column_key, plane_res, column_res, plane_got, column_got, total,
    partial, load_sem, plane_send, plane_recv, pass_send, pass_recv,
    column_send, column_recv, plane_key_send, plane_key_recv, column_key_send, column_key_recv,
    plane_res_send, plane_res_recv, column_res_send, column_res_recv,
):
    items, width = embeds_ref.shape
    lanes = plane_key.shape[2]
    slots = layers // 2
    cut = width // 4 * 3
    parts = [(0, cut), (cut, width - cut)]
    batch = batch_of(slots)
    batches = slots // batch if slots else 1
    g, d = lax.axis_index("grp"), lax.axis_index("dev")
    z, c = d // 2, d % 2

    def at(group, layer, core):
        return {"grp": group, "dev": layer * 2 + core}

    def group_up(s):
        return (g + s) % groups

    def layer_up(s):
        return (z + s) % layers

    def core(k):
        return (c + k) % 2

    def sends(s):
        return (s % 2 == 0) & (z + s < layers) | (s % 2 == 1) & (z + s >= layers)

    def first_odd(layer):
        return layer + 1 + layer % 2

    def slot_of(s):
        to = layer_up(s)
        return 1 + (1 - s % 2) * (s // 2 - 1) + (s % 2) * (to // 2 + (s - first_odd(to)) // 2)

    def offset_of(j):
        return jnp.where(j <= z // 2, 2 * j, first_odd(z) + 2 * (j - 1 - z // 2))

    def filled(j):
        return j <= z // 2 + (layers + 1 - first_odd(z)) // 2

    def remote(src, dst, send, recv, device):
        return pltpu.make_async_remote_copy(
            src_ref=src, dst_ref=dst, send_sem=send, recv_sem=recv,
            device_id=device, device_id_type=MESH,
        )

    def each(start, count, body):
        if count <= 4:
            for i in range(start, count):
                body(i)
        else:
            lax.fori_loop(start, count, lambda i, carry: (body(i), carry)[1], 0)

    def each_if(start, count, test, body):
        each(start, count, lambda i: pl.when(test(i))(lambda: body(i)))

    peers = range(1, groups)

    def plane_copy(s):
        return remote(embeds_hbm, plane.at[s], plane_send.at[s], plane_recv.at[s], at(group_up(s), z, c))

    def own_pass():
        return remote(embeds_hbm, column.at[0, 1], pass_send.at[0, 0], pass_recv.at[0, 0], at(g, z, core(1)))

    def pass_copy(j, h):
        columns = pl.ds(*parts[h])
        return remote(column.at[j, 0, :, columns], column.at[j, 1, :, columns],
                      pass_send.at[j, h], pass_recv.at[j, h], at(g, z, core(1)))

    def column_copy(s, j, h):
        columns = pl.ds(*parts[h])
        return remote(embeds_hbm.at[:, columns], column.at[j, 0, :, columns],
                      column_send.at[s, h], column_recv.at[j, h], at(g, layer_up(s), c))

    def plane_key_copy(s):
        return remote(plane_key.at[0], plane_key.at[s],
                      plane_key_send.at[s], plane_key_recv.at[s], at(group_up(s), z, c))

    def column_key_copy(s, j, k):
        return remote(plane_key.at[0], column_key.at[j, k],
                      column_key_send.at[s, k], column_key_recv.at[j, k], at(g, layer_up(s), core(k)))

    def plane_res_copy(s):
        return remote(plane_res.at[s], plane_got.at[s],
                      plane_res_send.at[s], plane_res_recv.at[s], at((g + groups - s) % groups, z, c))

    def column_res_copy(j, s, k):
        return remote(column_res.at[j, k], column_got.at[s, k],
                      column_res_send.at[j, k], column_res_recv.at[s, k],
                      at(g, (z + layers - s) % layers, core(k)))

    loads = [
        pltpu.make_async_copy(src, dst, load_sem.at[i])
        for i, (src, dst) in enumerate(
            [(embeds_hbm, embeds_ref), (cluster_hbm, cluster_ref), (priority_hbm, priority_ref)]
        )
    ]
    for load in loads:
        load.start()

    barrier = pltpu.get_barrier_semaphore()

    def greet(device):
        pl.semaphore_signal(barrier, inc=1, device_id=device, device_id_type=MESH)

    column_key[...] = jnp.full(column_key.shape, -2.0, jnp.float32)
    for k in range(2):
        each(1, layers, lambda s: greet(at(g, layer_up(s), core(k))))
    for s in peers:
        greet(at(group_up(s), z, c))
    greet(at(g, z, core(1)))
    pl.semaphore_wait(barrier, groups + 2 * (layers - 1))

    for h in range(2):
        each_if(1, layers, sends, lambda s: column_copy(s, slot_of(s), h).start())
    for s in peers:
        plane_copy(s).start()
    own_pass().start()

    total[...] = jnp.full(total.shape, -1.0, jnp.float32)
    plane_key[0] = jnp.full((8, lanes), -1.0, jnp.float32)
    for load in loads:
        load.wait()
    values = embeds_ref[...].astype(jnp.float32)
    scale = lax.rsqrt(jnp.sum(values * values, axis=1, keepdims=True) + 1e-06)
    normal[0] = (values * scale).astype(jnp.bfloat16)
    plane_key[0, 0:1, :items] = cluster_ref[...].reshape(1, items).astype(jnp.float32)
    plane_key[0, 1:2, :items] = priority_ref[...].reshape(1, items).astype(jnp.float32)
    plane_key[0, 2:3, :items] = jnp.broadcast_to(scale, (items, LANES)).T[0:1]
    for k in range(2):
        each_if(1, layers, sends, lambda s: column_key_copy(s, slot_of(s), k).start())
    for s in peers:
        plane_key_copy(s).start()
    column_key_copy(0, 0, 1).start()

    def column_keys(key):
        key = key.T[:items]
        return key[:, 0:1], key[:, 1:2], key[:, 2:3]

    def lane_keys(i):
        return jnp.concatenate([plane_key[s, i:i + 1, :items] for s in range(groups)], axis=1)

    def scaled(rows, scale):
        return (rows.astype(jnp.float32) * scale).astype(jnp.bfloat16)

    def hand_on(j, h):
        def one(slot):
            column_copy(1, slot, h).wait_recv()
            pass_copy(slot, h).start()
        for i in range(batch):
            pl.when(filled(1 + j * batch + i))(functools.partial(one, 1 + j * batch + i))

    def arrive(j, h):
        def wait(slot):
            pass_copy(slot, h).wait_recv()
            if h == 0:
                for k in range(2):
                    column_key_copy(1, slot, k).wait_recv()
        for i in range(batch):
            pl.when(filled(1 + j * batch + i))(functools.partial(wait, 1 + j * batch + i))

    def blocks_of(j):
        return [(0, 1)] + [(1 + j * batch + i, k) for i in range(batch) for k in range(2)]

    def part_product(j, h, scales):
        start, size = parts[h]
        here = slice(start, start + size)
        rows = [normal[0, :, here]]
        rows += [scaled(column[slot, k, :, here], scale) for (slot, k), scale in zip(blocks_of(j), scales)]
        return lax.dot_general(
            jnp.concatenate(rows, axis=0), normal[:, :, here].reshape(groups * items, size),
            (((1,), (1,)), ((), ())), preferred_element_type=jnp.float32,
        )

    def meet(j):
        arrive(j, 0)
        keys = [column_keys(plane_key[0])] + [column_keys(column_key[slot, k]) for slot, k in blocks_of(j)]
        scales = [key[2] for key in keys[1:]]
        partial[...] = part_product(j, 0, scales)
        cluster, rank = (jnp.concatenate([key[i] for key in keys], axis=0) for i in range(2))
        plane_cluster, plane_rank = lane_keys(0), lane_keys(1)
        arrive(j, 1)
        scores = partial[...] + part_product(j, 1, scales)
        scores = jnp.where(cluster == plane_cluster, scores, -1.0)
        earlier = plane_rank < rank
        ahead = jnp.where(earlier, scores, -1.0)
        fold = ahead[:, :LANES]
        for start in range(LANES, ahead.shape[1], LANES):
            fold = jnp.maximum(fold, ahead[:, start:start + LANES])

        def best_of(i):
            return jnp.max(fold[i * items:(i + 1) * items].T, axis=0, keepdims=True)

        for i, (slot, k) in reversed(list(enumerate(blocks_of(j), 1))):
            column_res[slot, k, 0:1, :items] = best_of(i)
            if i > 1:
                def send(slot, k):
                    column_res_copy(slot, offset_of(slot), k).start()
                pl.when(filled(slot))(functools.partial(send, slot, k))
        if batch:
            behind = jnp.where(earlier[2 * items:], -1.0, scores[2 * items:])
            total[0:1] = jnp.maximum(total[0:1], jnp.max(behind, axis=0, keepdims=True))
        if batches == 1:
            send_plane()
        column_res[0, 0, 0:1, :items] = best_of(0)

    def send_plane():
        for s in range(groups):
            plane_res[s, 0:1, :items] = total[0:1, s * items:(s + 1) * items]
        for s in peers:
            plane_res_copy(s).start()
        column_res_copy(0, 0, 1).start()

    own_pass().wait_recv()
    column_key_copy(0, 0, 1).wait_recv()
    for s in peers:
        plane_key_copy(s).wait_recv()
    each(0, batches, lambda j: hand_on(j, 0))
    for s in peers:
        plane_copy(s).wait_recv()
        normal[s] = scaled(plane[s], column_keys(plane_key[s])[2])
    each(0, batches, lambda j: hand_on(j, 1))
    each(0, batches, meet)
    if batches > 1:
        send_plane()

    best = jnp.maximum(column_res[0, 0, 0:1, :items], plane_res[0, 0:1, :items])
    column_res_copy(0, 0, 1).wait_recv()
    best = jnp.maximum(best, column_got[0, 1, 0:1, :items])
    for s in peers:
        plane_res_copy(s).wait_recv()
        best = jnp.maximum(best, plane_got[s, 0:1, :items])
    total[0:1, :items] = best

    def take_column(s):
        for k in range(2):
            column_res_copy(0, s, k).wait_recv()
            total[0:1, :items] = jnp.maximum(total[0:1, :items], column_got[s, k, 0:1, :items])

    each_if(1, layers, sends, take_column)
    out_ref[...] = total[0:1, :items].reshape(items)

    for s in peers:
        plane_copy(s).wait_send()
        plane_key_copy(s).wait_send()
        plane_res_copy(s).wait_send()
    own_pass().wait_send()
    column_key_copy(0, 0, 1).wait_send()
    column_res_copy(0, 0, 1).wait_send()

    def sent_out(s):
        for i in range(2):
            column_copy(s, 0, i).wait_send()
            column_key_copy(s, 0, i).wait_send()

    def sent_in(j):
        for i in range(2):
            pass_copy(j, i).wait_send()
            column_res_copy(j, 1, i).wait_send()

    each_if(1, layers, sends, sent_out)
    each_if(1, slots + 1, filled, sent_in)


def per_device(embeds, cluster, priority):
    groups, layers = lax.axis_size("grp"), lax.axis_size("dev") // 2
    slots = layers // 2
    items, width = embeds.shape
    lanes = -(-items // LANES) * LANES
    blocks = 2 * (1 + batch_of(slots))
    dma = pltpu.SemaphoreType.DMA
    return pl.pallas_call(
        functools.partial(kernel, groups, layers),
        out_shape=jax.ShapeDtypeStruct((items,), jnp.float32),
        in_specs=[pl.BlockSpec(memory_space=pltpu.HBM)] * 3,
        out_specs=pl.BlockSpec(memory_space=pltpu.VMEM),
        scratch_shapes=[
            pltpu.VMEM((items, width), jnp.bfloat16),
            pltpu.VMEM((items,), jnp.int32),
            pltpu.VMEM((items,), jnp.int32),
            pltpu.VMEM((groups, items, width), jnp.bfloat16),
            pltpu.VMEM((groups, items, width), jnp.bfloat16),
            pltpu.VMEM((slots + 1, 2, items, width), jnp.bfloat16),
            pltpu.VMEM((groups, 8, lanes), jnp.float32),
            pltpu.VMEM((slots + 1, 2, 8, lanes), jnp.float32),
            pltpu.VMEM((groups, 8, lanes), jnp.float32),
            pltpu.VMEM((slots + 1, 2, 8, lanes), jnp.float32),
            pltpu.VMEM((groups, 8, lanes), jnp.float32),
            pltpu.VMEM((layers, 2, 8, lanes), jnp.float32),
            pltpu.VMEM((8, groups * items), jnp.float32),
            pltpu.VMEM((blocks * items, groups * items), jnp.float32),
            dma((3,)),
            dma((groups,)), dma((groups,)),
            dma((slots + 1, 2)), dma((slots + 1, 2)),
            dma((layers, 2)), dma((slots + 1, 2)),
            dma((groups,)), dma((groups,)),
            dma((layers, 2)), dma((slots + 1, 2)),
            dma((groups,)), dma((groups,)),
            dma((slots + 1, 2)), dma((layers, 2)),
        ],
        compiler_params=pltpu.CompilerParams(
            collective_id=0, has_side_effects=True, vmem_limit_bytes=40 * 1024 * 1024
        ),
    )(*[pltpu.with_memory_space_constraint(x, pltpu.HBM) for x in (embeds, cluster, priority)])


def solution(mesh):
    in_specs = (P(("grp", "dev"), None), P(("grp", "dev")), P(("grp", "dev")))
    out_specs = P(("grp", "dev"))
    return jax.shard_map(
        per_device, mesh=mesh, in_specs=in_specs, out_specs=out_specs, check_vma=False
    )
```

```python
import functools

import jax
import jax.numpy as jnp
from jax import lax
from jax.experimental import pallas as pl
from jax.experimental.pallas import tpu as pltpu
from jax.sharding import PartitionSpec as P

MESH = pl.DeviceIdType.MESH
LANES = 128


def batch_of(slots):
    return 0 if slots == 0 else 2 if slots % 2 == 0 else 1


def kernel(
    groups, layers, embeds_hbm, cluster_hbm, priority_hbm, out_ref,
    embeds_ref, cluster_ref, priority_ref,
    plane, normal, column, plane_key, column_key, plane_res, column_res, plane_got, column_got, total,
    partial, load_sem, plane_send, plane_recv, pass_send, pass_recv,
    column_send, column_recv, plane_key_send, plane_key_recv, column_key_send, column_key_recv,
    plane_res_send, plane_res_recv, column_res_send, column_res_recv,
):
    items, width = embeds_ref.shape
    lanes = plane_key.shape[2]
    slots = layers // 2
    cut = width // 4 * 3
    parts = [(0, cut), (cut, width - cut)]
    batch = batch_of(slots)
    batches = slots // batch if slots else 1
    g, d = lax.axis_index("grp"), lax.axis_index("dev")
    z, c = d // 2, d % 2

    def at(group, layer, core):
        return {"grp": group, "dev": layer * 2 + core}

    def group_up(s):
        return (g + s) % groups

    def layer_up(s):
        return (z + s) % layers

    def core(k):
        return (c + k) % 2

    def sends(s):
        return (s % 2 == 0) & (z + s < layers) | (s % 2 == 1) & (z + s >= layers)

    def first_odd(layer):
        return layer + 1 + layer % 2

    def slot_of(s):
        to = layer_up(s)
        return 1 + (1 - s % 2) * (s // 2 - 1) + (s % 2) * (to // 2 + (s - first_odd(to)) // 2)

    def offset_of(j):
        return jnp.where(j <= z // 2, 2 * j, first_odd(z) + 2 * (j - 1 - z // 2))

    def filled(j):
        return j <= z // 2 + (layers + 1 - first_odd(z)) // 2

    def remote(src, dst, send, recv, device):
        return pltpu.make_async_remote_copy(
            src_ref=src, dst_ref=dst, send_sem=send, recv_sem=recv,
            device_id=device, device_id_type=MESH,
        )

    def each(start, count, body):
        if count <= 4:
            for i in range(start, count):
                body(i)
        else:
            lax.fori_loop(start, count, lambda i, carry: (body(i), carry)[1], 0)

    def each_if(start, count, test, body):
        each(start, count, lambda i: pl.when(test(i))(lambda: body(i)))

    peers = range(1, groups)

    def plane_copy(s):
        return remote(embeds_ref, plane.at[s], plane_send.at[s], plane_recv.at[s], at(group_up(s), z, c))

    def own_pass():
        return remote(embeds_ref, column.at[0, 1], pass_send.at[0, 0], pass_recv.at[0, 0], at(g, z, core(1)))

    def pass_copy(j, h):
        columns = pl.ds(*parts[h])
        return remote(column.at[j, 0, :, columns], column.at[j, 1, :, columns],
                      pass_send.at[j, h], pass_recv.at[j, h], at(g, z, core(1)))

    def column_copy(s, j, h):
        columns = pl.ds(*parts[h])
        return remote(embeds_ref.at[:, columns], column.at[j, 0, :, columns],
                      column_send.at[s, h], column_recv.at[j, h], at(g, layer_up(s), c))

    def plane_key_copy(s):
        return remote(plane_key.at[0], plane_key.at[s],
                      plane_key_send.at[s], plane_key_recv.at[s], at(group_up(s), z, c))

    def column_key_copy(s, j, k):
        return remote(plane_key.at[0], column_key.at[j, k],
                      column_key_send.at[s, k], column_key_recv.at[j, k], at(g, layer_up(s), core(k)))

    def plane_res_copy(s):
        return remote(plane_res.at[s], plane_got.at[s],
                      plane_res_send.at[s], plane_res_recv.at[s], at((g + groups - s) % groups, z, c))

    def column_res_copy(j, s, k):
        return remote(column_res.at[j, k], column_got.at[s, k],
                      column_res_send.at[j, k], column_res_recv.at[s, k],
                      at(g, (z + layers - s) % layers, core(k)))

    loads = [
        pltpu.make_async_copy(src, dst, load_sem.at[i])
        for i, (src, dst) in enumerate(
            [(embeds_hbm, embeds_ref), (cluster_hbm, cluster_ref), (priority_hbm, priority_ref)]
        )
    ]
    for load in loads:
        load.start()

    barrier = pltpu.get_barrier_semaphore()

    def greet(device):
        pl.semaphore_signal(barrier, inc=1, device_id=device, device_id_type=MESH)

    column_key[...] = jnp.full(column_key.shape, -2.0, jnp.float32)
    for k in range(2):
        each(1, layers, lambda s: greet(at(g, layer_up(s), core(k))))
    for s in peers:
        greet(at(group_up(s), z, c))
    greet(at(g, z, core(1)))
    pl.semaphore_wait(barrier, groups + 2 * (layers - 1))

    for load in loads:
        load.wait()
    for h in range(2):
        each_if(1, layers, sends, lambda s: column_copy(s, slot_of(s), h).start())
    for s in peers:
        plane_copy(s).start()
    own_pass().start()

    total[...] = jnp.full(total.shape, -1.0, jnp.float32)
    plane_key[0] = jnp.full((8, lanes), -1.0, jnp.float32)
    values = embeds_ref[...].astype(jnp.float32)
    scale = lax.rsqrt(jnp.sum(values * values, axis=1, keepdims=True) + 1e-06)
    normal[0] = (values * scale).astype(jnp.bfloat16)
    plane_key[0, 0:1, :items] = cluster_ref[...].reshape(1, items).astype(jnp.float32)
    plane_key[0, 1:2, :items] = priority_ref[...].reshape(1, items).astype(jnp.float32)
    plane_key[0, 2:3, :items] = jnp.broadcast_to(scale, (items, LANES)).T[0:1]
    for k in range(2):
        each_if(1, layers, sends, lambda s: column_key_copy(s, slot_of(s), k).start())
    for s in peers:
        plane_key_copy(s).start()
    column_key_copy(0, 0, 1).start()

    def column_keys(key):
        key = key.T[:items]
        return key[:, 0:1], key[:, 1:2], key[:, 2:3]

    def lane_keys(i):
        return jnp.concatenate([plane_key[s, i:i + 1, :items] for s in range(groups)], axis=1)

    def scaled(rows, scale):
        return (rows.astype(jnp.float32) * scale).astype(jnp.bfloat16)

    def hand_on(j, h):
        def one(slot):
            column_copy(1, slot, h).wait_recv()
            pass_copy(slot, h).start()
        for i in range(batch):
            pl.when(filled(1 + j * batch + i))(functools.partial(one, 1 + j * batch + i))

    def arrive(j, h):
        def wait(slot):
            pass_copy(slot, h).wait_recv()
            if h == 0:
                for k in range(2):
                    column_key_copy(1, slot, k).wait_recv()
        for i in range(batch):
            pl.when(filled(1 + j * batch + i))(functools.partial(wait, 1 + j * batch + i))

    def blocks_of(j):
        return [(0, 1)] + [(1 + j * batch + i, k) for i in range(batch) for k in range(2)]

    def part_product(j, h, scales):
        start, size = parts[h]
        here = slice(start, start + size)
        rows = [normal[0, :, here]]
        rows += [scaled(column[slot, k, :, here], scale) for (slot, k), scale in zip(blocks_of(j), scales)]
        return lax.dot_general(
            jnp.concatenate(rows, axis=0), normal[:, :, here].reshape(groups * items, size),
            (((1,), (1,)), ((), ())), preferred_element_type=jnp.float32,
        )

    def meet(j):
        arrive(j, 0)
        keys = [column_keys(plane_key[0])] + [column_keys(column_key[slot, k]) for slot, k in blocks_of(j)]
        scales = [key[2] for key in keys[1:]]
        partial[...] = part_product(j, 0, scales)
        cluster, rank = (jnp.concatenate([key[i] for key in keys], axis=0) for i in range(2))
        plane_cluster, plane_rank = lane_keys(0), lane_keys(1)
        arrive(j, 1)
        scores = partial[...] + part_product(j, 1, scales)
        scores = jnp.where(cluster == plane_cluster, scores, -1.0)
        earlier = plane_rank < rank
        ahead = jnp.where(earlier, scores, -1.0)
        fold = ahead[:, :LANES]
        for start in range(LANES, ahead.shape[1], LANES):
            fold = jnp.maximum(fold, ahead[:, start:start + LANES])

        def best_of(i):
            return jnp.max(fold[i * items:(i + 1) * items].T, axis=0, keepdims=True)

        for i, (slot, k) in reversed(list(enumerate(blocks_of(j), 1))):
            column_res[slot, k, 0:1, :items] = best_of(i)
            if i > 1:
                def send(slot, k):
                    column_res_copy(slot, offset_of(slot), k).start()
                pl.when(filled(slot))(functools.partial(send, slot, k))
        if batch:
            behind = jnp.where(earlier[2 * items:], -1.0, scores[2 * items:])
            total[0:1] = jnp.maximum(total[0:1], jnp.max(behind, axis=0, keepdims=True))
        if batches == 1:
            send_plane()
        column_res[0, 0, 0:1, :items] = best_of(0)

    def send_plane():
        for s in range(groups):
            plane_res[s, 0:1, :items] = total[0:1, s * items:(s + 1) * items]
        for s in peers:
            plane_res_copy(s).start()
        column_res_copy(0, 0, 1).start()

    own_pass().wait_recv()
    column_key_copy(0, 0, 1).wait_recv()
    for s in peers:
        plane_key_copy(s).wait_recv()
    each(0, batches, lambda j: hand_on(j, 0))
    for s in peers:
        plane_copy(s).wait_recv()
        normal[s] = scaled(plane[s], column_keys(plane_key[s])[2])
    each(0, batches, lambda j: hand_on(j, 1))
    each(0, batches, meet)
    if batches > 1:
        send_plane()

    best = jnp.maximum(column_res[0, 0, 0:1, :items], plane_res[0, 0:1, :items])
    column_res_copy(0, 0, 1).wait_recv()
    best = jnp.maximum(best, column_got[0, 1, 0:1, :items])
    for s in peers:
        plane_res_copy(s).wait_recv()
        best = jnp.maximum(best, plane_got[s, 0:1, :items])
    total[0:1, :items] = best

    def take_column(s):
        for k in range(2):
            column_res_copy(0, s, k).wait_recv()
            total[0:1, :items] = jnp.maximum(total[0:1, :items], column_got[s, k, 0:1, :items])

    each_if(1, layers, sends, take_column)
    out_ref[...] = total[0:1, :items].reshape(items)

    for s in peers:
        plane_copy(s).wait_send()
        plane_key_copy(s).wait_send()
        plane_res_copy(s).wait_send()
    own_pass().wait_send()
    column_key_copy(0, 0, 1).wait_send()
    column_res_copy(0, 0, 1).wait_send()

    def sent_out(s):
        for i in range(2):
            column_copy(s, 0, i).wait_send()
            column_key_copy(s, 0, i).wait_send()

    def sent_in(j):
        for i in range(2):
            pass_copy(j, i).wait_send()
            column_res_copy(j, 1, i).wait_send()

    each_if(1, layers, sends, sent_out)
    each_if(1, slots + 1, filled, sent_in)


def per_device(embeds, cluster, priority):
    groups, layers = lax.axis_size("grp"), lax.axis_size("dev") // 2
    slots = layers // 2
    items, width = embeds.shape
    lanes = -(-items // LANES) * LANES
    blocks = 2 * (1 + batch_of(slots))
    dma = pltpu.SemaphoreType.DMA
    return pl.pallas_call(
        functools.partial(kernel, groups, layers),
        out_shape=jax.ShapeDtypeStruct((items,), jnp.float32),
        in_specs=[pl.BlockSpec(memory_space=pltpu.HBM)] * 3,
        out_specs=pl.BlockSpec(memory_space=pltpu.VMEM),
        scratch_shapes=[
            pltpu.VMEM((items, width), jnp.bfloat16),
            pltpu.VMEM((items,), jnp.int32),
            pltpu.VMEM((items,), jnp.int32),
            pltpu.VMEM((groups, items, width), jnp.bfloat16),
            pltpu.VMEM((groups, items, width), jnp.bfloat16),
            pltpu.VMEM((slots + 1, 2, items, width), jnp.bfloat16),
            pltpu.VMEM((groups, 8, lanes), jnp.float32),
            pltpu.VMEM((slots + 1, 2, 8, lanes), jnp.float32),
            pltpu.VMEM((groups, 8, lanes), jnp.float32),
            pltpu.VMEM((slots + 1, 2, 8, lanes), jnp.float32),
            pltpu.VMEM((groups, 8, lanes), jnp.float32),
            pltpu.VMEM((layers, 2, 8, lanes), jnp.float32),
            pltpu.VMEM((8, groups * items), jnp.float32),
            pltpu.VMEM((blocks * items, groups * items), jnp.float32),
            dma((3,)),
            dma((groups,)), dma((groups,)),
            dma((slots + 1, 2)), dma((slots + 1, 2)),
            dma((layers, 2)), dma((slots + 1, 2)),
            dma((groups,)), dma((groups,)),
            dma((layers, 2)), dma((slots + 1, 2)),
            dma((groups,)), dma((groups,)),
            dma((slots + 1, 2)), dma((layers, 2)),
        ],
        compiler_params=pltpu.CompilerParams(
            collective_id=0, has_side_effects=True, vmem_limit_bytes=40 * 1024 * 1024
        ),
    )(*[pltpu.with_memory_space_constraint(x, pltpu.HBM) for x in (embeds, cluster, priority)])


def solution(mesh):
    in_specs = (P(("grp", "dev"), None), P(("grp", "dev")), P(("grp", "dev")))
    out_specs = P(("grp", "dev"))
    return jax.shard_map(
        per_device, mesh=mesh, in_specs=in_specs, out_specs=out_specs, check_vma=False
    )
```

```python
import functools

import jax
import jax.numpy as jnp
from jax import lax
from jax.experimental import pallas as pl
from jax.experimental.pallas import tpu as pltpu
from jax.sharding import PartitionSpec as P

MESH = pl.DeviceIdType.MESH
LANES = 128


def batch_of(slots):
    return 0 if slots == 0 else 2 if slots % 2 == 0 else 1


def kernel(
    groups, layers, embeds_hbm, cluster_hbm, priority_hbm, out_ref,
    embeds_ref, cluster_ref, priority_ref,
    plane, normal, column, plane_key, column_key, plane_res, column_res, plane_got, column_got, total,
    own_res, partial, load_sem, plane_send, plane_recv, relay_send, relay_recv, pass_send, pass_recv,
    column_send, column_recv, plane_key_send, plane_key_recv, column_key_send, column_key_recv,
    plane_res_send, plane_res_recv, column_res_send, column_res_recv,
):
    items, width = embeds_ref.shape
    lanes = plane_key.shape[3]
    slots = layers // 2
    half = items // 2
    cut = width // 4 * 3
    parts = [(0, cut), (cut, width - cut)]
    lows = 2 if groups % 2 == 0 else 1
    highs = groups // lows
    batch = batch_of(slots)
    batches = slots // batch if slots else 1
    g, d = lax.axis_index("grp"), lax.axis_index("dev")
    z, c = d // 2, d % 2

    def at(group, layer, core):
        return {"grp": group, "dev": layer * 2 + core}

    def group_up(s):
        high, low = s // lows, s % lows
        return (g // lows + high) % highs * lows + (g % lows + low) % lows

    def group_down(s):
        high, low = s // lows, s % lows
        return (g // lows + highs - high) % highs * lows + (g % lows + lows - low) % lows

    def layer_up(s):
        return (z + s) % layers

    def core(k):
        return (c + k) % 2

    def sends(s):
        return (s % 2 == 0) & (z + s < layers) | (s % 2 == 1) & (z + s >= layers)

    def first_odd(layer):
        return layer + 1 + layer % 2

    def slot_of(s):
        to = layer_up(s)
        return (1 - s % 2) * (s // 2 - 1) + (s % 2) * (to // 2 + (s - first_odd(to)) // 2)

    def offset_of(j):
        return jnp.where(j < z // 2, 2 * (j + 1), first_odd(z) + 2 * (j - z // 2))

    def filled(j):
        return j < z // 2 + (layers + 1 - first_odd(z)) // 2

    def remote(src, dst, send, recv, device):
        return pltpu.make_async_remote_copy(
            src_ref=src, dst_ref=dst, send_sem=send, recv_sem=recv,
            device_id=device, device_id_type=MESH,
        )

    def each(start, count, body):
        if count <= 4:
            for i in range(start, count):
                body(i)
        else:
            lax.fori_loop(start, count, lambda i, carry: (body(i), carry)[1], 0)

    def each_if(start, count, test, body):
        each(start, count, lambda i: pl.when(test(i))(lambda: body(i)))

    near = [s for s in range(1, groups) if s < lows or s % lows == 0]
    far = [s for s in range(1, groups) if s not in near]
    every = [(s, k) for s in range(groups) for k in range(2)]
    peers = every[1:]

    def rows_of(h):
        return pl.ds(h * half, half)

    def plane_copy(s, h):
        return remote(embeds_hbm.at[rows_of(h)], plane.at[s, 0, rows_of(h)],
                      plane_send.at[s, h], plane_recv.at[s, h], at(group_up(s), z, c))

    def relay_copy(s, h):
        low, high = s % lows, s - s % lows
        source, way = (low, high) if h == 0 else (high, low)
        return remote(plane.at[source, 0, rows_of(h)], plane.at[s, 0, rows_of(h)],
                      relay_send.at[s, h], relay_recv.at[s, h], at(group_up(way), z, c))

    def pass_copy(s, h):
        rows = rows_of(h)
        return remote(plane.at[s, 0, rows] if s else embeds_hbm.at[rows], plane.at[s, 1, rows],
                      pass_send.at[s, h], pass_recv.at[s, h], at(g, z, core(1)))

    def column_copy(s, j, h):
        columns = pl.ds(*parts[h])
        return remote(embeds_hbm.at[:, columns], column.at[j, :, columns],
                      column_send.at[s, h], column_recv.at[j, h], at(g, layer_up(s), c))

    def plane_key_copy(s, k):
        return remote(plane_key.at[0, 0], plane_key.at[s, k],
                      plane_key_send.at[s, k], plane_key_recv.at[s, k], at(group_up(s), z, core(k)))

    def column_key_copy(s, j):
        return remote(plane_key.at[0, 0], column_key.at[j],
                      column_key_send.at[s], column_key_recv.at[j], at(g, layer_up(s), c))

    def plane_res_copy(s, k):
        return remote(plane_res.at[s, k], plane_got.at[s, k],
                      plane_res_send.at[s, k], plane_res_recv.at[s, k], at(group_down(s), z, core(k)))

    def column_res_copy(j, s):
        return remote(column_res.at[j], column_got.at[s],
                      column_res_send.at[j], column_res_recv.at[s], at(g, (z + layers - s) % layers, c))

    loads = [
        pltpu.make_async_copy(src, dst, load_sem.at[i])
        for i, (src, dst) in enumerate(
            [(embeds_hbm, embeds_ref), (cluster_hbm, cluster_ref), (priority_hbm, priority_ref)]
        )
    ]
    for load in loads:
        load.start()

    barrier = pltpu.get_barrier_semaphore()

    def greet(device):
        pl.semaphore_signal(barrier, inc=1, device_id=device, device_id_type=MESH)

    column_key[...] = jnp.full(column_key.shape, -2.0, jnp.float32)
    each(1, layers, lambda s: greet(at(g, layer_up(s), c)))
    for s, k in peers:
        greet(at(group_up(s), z, core(k)))

    pl.semaphore_wait(barrier, len(peers) + layers - 1)

    def first_half(s):
        return 0 if s < lows else 1

    for i in range(2):
        for s in near:
            plane_copy(s, first_half(s) if i == 0 else 1 - first_half(s)).start()
        each_if(1, layers, sends, lambda s: column_copy(s, slot_of(s), i).start())
    for h in range(2):
        pass_copy(0, h).start()

    total[...] = jnp.full(total.shape, -1.0, jnp.float32)
    plane_key[0, 0] = jnp.full((8, lanes), -1.0, jnp.float32)
    for load in loads:
        load.wait()
    values = embeds_ref[...].astype(jnp.float32)
    scale = lax.rsqrt(jnp.sum(values * values, axis=1, keepdims=True) + 1e-06)
    normal[0, 0] = (values * scale).astype(jnp.bfloat16)
    plane_key[0, 0, 0:1, :items] = cluster_ref[...].reshape(1, items).astype(jnp.float32)
    plane_key[0, 0, 1:2, :items] = priority_ref[...].reshape(1, items).astype(jnp.float32)
    plane_key[0, 0, 2:3, :items] = jnp.broadcast_to(scale, (items, LANES)).T[0:1]
    for s, k in peers:
        plane_key_copy(s, k).start()
    each_if(1, layers, sends, lambda s: column_key_copy(s, slot_of(s)).start())

    for s in near:
        plane_copy(s, first_half(s)).wait_recv()
        for t in far:
            if s == t % lows:
                relay_copy(t, 0).start()
            if s == t - t % lows:
                relay_copy(t, 1).start()
        pass_copy(s, first_half(s)).start()

    def column_keys(key):
        key = key.T[:items]
        return key[:, 0:1], key[:, 1:2], key[:, 2:3]

    def lane_keys(blocks, i):
        return jnp.concatenate([plane_key[s, k, i:i + 1, :items] for s, k in blocks], axis=1)

    def product(rows, others):
        return lax.dot_general(
            rows, others, (((1,), (1,)), ((), ())), preferred_element_type=jnp.float32
        )

    def scaled(rows, scale):
        return (rows.astype(jnp.float32) * scale).astype(jnp.bfloat16)

    def scale_plane(s, k):
        normal[s, k] = scaled(plane[s, k], column_keys(plane_key[s, k])[2])

    def arrive(j, h):
        def wait(i):
            column_copy(1, i, h).wait_recv()
            if h == 0:
                column_key_copy(1, i).wait_recv()
        for i in range(batch):
            pl.when(filled(j * batch + i))(functools.partial(wait, j * batch + i))

    def part_product(j, h, scales):
        start, size = parts[h]
        here = slice(start, start + size)
        rows = [normal[0, 0, :, here]]
        rows += [scaled(column[j * batch + i, :, here], scales[i]) for i in range(batch)]
        return product(jnp.concatenate(rows, axis=0), normal[:, :, :, here].reshape(len(every) * items, size))

    def meet(j):
        arrive(j, 0)
        keys = [column_keys(plane_key[0, 0])] + [column_keys(column_key[j * batch + i]) for i in range(batch)]
        scales = [key[2] for key in keys[1:]]
        partial[...] = part_product(j, 0, scales)
        cluster, rank = (jnp.concatenate([key[i] for key in keys], axis=0) for i in range(2))
        plane_cluster, plane_rank = lane_keys(every, 0), lane_keys(every, 1)
        arrive(j, 1)
        scores = partial[...] + part_product(j, 1, scales)
        scores = jnp.where(cluster == plane_cluster, scores, -1.0)
        earlier = plane_rank < rank
        if batch:
            behind = jnp.where(earlier[items:], -1.0, scores[items:])
            total[0:1] = jnp.maximum(total[0:1], jnp.max(behind, axis=0, keepdims=True))
        if batches == 1:
            send_plane()
        ahead = jnp.where(earlier, scores, -1.0)
        fold = ahead[:, :LANES]
        for start in range(LANES, ahead.shape[1], LANES):
            fold = jnp.maximum(fold, ahead[:, start:start + LANES])

        def best_of(i):
            return jnp.max(fold[i * items:(i + 1) * items].T, axis=0, keepdims=True)

        for i in range(batch):
            column_res[j * batch + i, 0:1, :items] = best_of(1 + i)

            def send(slot):
                column_res_copy(slot, offset_of(slot)).start()
            pl.when(filled(j * batch + i))(functools.partial(send, j * batch + i))
        own_res[0:1, :items] = best_of(0)

    def send_plane():
        for b, (s, k) in enumerate(every):
            plane_res[s, k, 0:1, :items] = total[0:1, b * items:(b + 1) * items]
        for s, k in reversed(peers):
            plane_res_copy(s, k).start()

    def passed(s):
        for h in range(2):
            pass_copy(s, h).wait_recv()
        scale_plane(s, 1)

    for s, k in peers:
        plane_key_copy(s, k).wait_recv()
    passed(0)
    for s in near:
        plane_copy(s, 1 - first_half(s)).wait_recv()
        pass_copy(s, 1 - first_half(s)).start()
        scale_plane(s, 0)
    for s in far:
        for h in range(2):
            relay_copy(s, h).wait_recv()
            pass_copy(s, h).start()
        scale_plane(s, 0)
    for s in near + far:
        passed(s)
    if batches == 1:
        meet(0)
    else:
        each(0, batches, meet)
        send_plane()

    best = own_res[0:1, :items]
    best = jnp.maximum(best, plane_res[0, 0, 0:1, :items])
    for s, k in peers:
        plane_res_copy(s, k).wait_recv()
        best = jnp.maximum(best, plane_got[s, k, 0:1, :items])
    total[0:1, :items] = best

    def take_column(s):
        column_res_copy(0, s).wait_recv()
        total[0:1, :items] = jnp.maximum(total[0:1, :items], column_got[s, 0:1, :items])

    each_if(1, layers, sends, take_column)
    out_ref[...] = total[0:1, :items].reshape(items)

    for s in near:
        for h in range(2):
            plane_copy(s, h).wait_send()
    for s in far:
        for h in range(2):
            relay_copy(s, h).wait_send()
    for s in range(groups):
        for h in range(2):
            pass_copy(s, h).wait_send()
    for s, k in peers:
        plane_key_copy(s, k).wait_send()
        plane_res_copy(s, k).wait_send()

    def sent_out(s):
        for h in range(2):
            column_copy(s, 0, h).wait_send()
        column_key_copy(s, 0).wait_send()

    each_if(1, layers, sends, sent_out)
    each_if(0, slots, filled, lambda j: column_res_copy(j, 1).wait_send())


def per_device(embeds, cluster, priority):
    groups, layers = lax.axis_size("grp"), lax.axis_size("dev") // 2
    slots = layers // 2
    items, width = embeds.shape
    lanes = -(-items // LANES) * LANES
    batch = batch_of(slots)
    dma = pltpu.SemaphoreType.DMA
    some = max(slots, 1)
    return pl.pallas_call(
        functools.partial(kernel, groups, layers),
        out_shape=jax.ShapeDtypeStruct((items,), jnp.float32),
        in_specs=[pl.BlockSpec(memory_space=pltpu.HBM)] * 3,
        out_specs=pl.BlockSpec(memory_space=pltpu.VMEM),
        scratch_shapes=[
            pltpu.VMEM((items, width), jnp.bfloat16),
            pltpu.VMEM((items,), jnp.int32),
            pltpu.VMEM((items,), jnp.int32),
            pltpu.VMEM((groups, 2, items, width), jnp.bfloat16),
            pltpu.VMEM((groups, 2, items, width), jnp.bfloat16),
            pltpu.VMEM((some, items, width), jnp.bfloat16),
            pltpu.VMEM((groups, 2, 8, lanes), jnp.float32),
            pltpu.VMEM((some, 8, lanes), jnp.float32),
            pltpu.VMEM((groups, 2, 8, lanes), jnp.float32),
            pltpu.VMEM((some, 8, lanes), jnp.float32),
            pltpu.VMEM((groups, 2, 8, lanes), jnp.float32),
            pltpu.VMEM((layers, 8, lanes), jnp.float32),
            pltpu.VMEM((8, groups * 2 * items), jnp.float32),
            pltpu.VMEM((8, lanes), jnp.float32),
            pltpu.VMEM(((1 + batch) * items, groups * 2 * items), jnp.float32),
            dma((3,)),
            dma((groups, 2)), dma((groups, 2)),
            dma((groups, 2)), dma((groups, 2)),
            dma((groups, 2)), dma((groups, 2)),
            dma((layers, 2)), dma((some, 2)),
            dma((groups, 2)), dma((groups, 2)),
            dma((layers,)), dma((some,)),
            dma((groups, 2)), dma((groups, 2)),
            dma((some,)), dma((layers,)),
        ],
        compiler_params=pltpu.CompilerParams(
            collective_id=0, has_side_effects=True, vmem_limit_bytes=40 * 1024 * 1024
        ),
    )(*[pltpu.with_memory_space_constraint(x, pltpu.HBM) for x in (embeds, cluster, priority)])


def solution(mesh):
    in_specs = (P(("grp", "dev"), None), P(("grp", "dev")), P(("grp", "dev")))
    out_specs = P(("grp", "dev"))
    return jax.shard_map(
        per_device, mesh=mesh, in_specs=in_specs, out_specs=out_specs, check_vma=False
    )
```

```python
import functools

import jax
import jax.numpy as jnp
from jax import lax
from jax.experimental import pallas as pl
from jax.experimental.pallas import tpu as pltpu
from jax.sharding import PartitionSpec as P

MESH = pl.DeviceIdType.MESH
LANES = 128


def kernel(
    groups, layers, embeds_hbm, cluster_hbm, priority_hbm, out_ref,
    embeds_ref, cluster_ref, priority_ref,
    plane, normal, column, plane_key, column_key, plane_res, column_res, plane_got, column_got, total,
    own_res, load_sem, plane_send, plane_recv, relay_send, relay_recv, pass_send, pass_recv,
    column_send, column_recv, plane_key_send, plane_key_recv, column_key_send, column_key_recv,
    plane_res_send, plane_res_recv, column_res_send, column_res_recv,
):
    items, width = embeds_ref.shape
    lanes = plane_key.shape[3]
    mid = layers // 2
    half = items // 2
    cut = width // 2
    parts = [(0, cut), (cut, width - cut)]
    lows = 2 if groups % 2 == 0 else 1
    highs = groups // lows
    g, d = lax.axis_index("grp"), lax.axis_index("dev")
    z, c = d // 2, d % 2

    def at(group, layer, core):
        return {"grp": group, "dev": layer * 2 + core}

    def group_up(s):
        high, low = s // lows, s % lows
        return (g // lows + high) % highs * lows + (g % lows + low) % lows

    def group_down(s):
        high, low = s // lows, s % lows
        return (g // lows + highs - high) % highs * lows + (g % lows + lows - low) % lows

    def layer_up(s):
        return (z + s) % layers

    def core(k):
        return (c + k) % 2

    def slot_of(a):
        return jnp.where(a < mid, a, a - 1)

    def takes(a):
        return (a < mid) & (z > a) | (a > mid) & (z >= mid) & (z < a)

    def gives(b):
        return (z < mid) & (b > z) | (z > mid) & (b >= mid) & (b < z)

    def onward(a):
        return (a < mid) & (z < layers - 1) | (a > mid) & (z > mid)

    def remote(src, dst, send, recv, device):
        return pltpu.make_async_remote_copy(
            src_ref=src, dst_ref=dst, send_sem=send, recv_sem=recv,
            device_id=device, device_id_type=MESH,
        )

    def each(start, count, body):
        if count <= 4:
            for i in range(start, count):
                body(i)
        else:
            lax.fori_loop(start, count, lambda i, carry: (body(i), carry)[1], 0)

    def each_if(start, count, test, body):
        each(start, count, lambda i: pl.when(test(i))(lambda: body(i)))

    near = [s for s in range(1, groups) if s < lows or s % lows == 0]
    far = [s for s in range(1, groups) if s not in near]
    every = [(s, k) for s in range(groups) for k in range(2)]
    peers = every[1:]

    def rows_of(h):
        return pl.ds(h * half, half)

    def plane_copy(s, h):
        return remote(embeds_hbm.at[rows_of(h)], plane.at[s, 0, rows_of(h)],
                      plane_send.at[s, h], plane_recv.at[s, h], at(group_up(s), z, c))

    def relay_copy(s, h):
        low, high = s % lows, s - s % lows
        source, way = (low, high) if h == 0 else (high, low)
        return remote(plane.at[source, 0, rows_of(h)], plane.at[s, 0, rows_of(h)],
                      relay_send.at[s, h], relay_recv.at[s, h], at(group_up(way), z, c))

    def pass_copy(s):
        return remote(plane.at[s, 0] if s else embeds_hbm, plane.at[s, 1],
                      pass_send.at[s], pass_recv.at[s], at(g, z, core(1)))

    def column_copy(a, h, own):
        columns = pl.ds(*parts[h])
        to = jnp.where(a < mid, lax.rem(z + 1, layers), lax.rem(z + layers - 1, layers))
        source = embeds_hbm if own else column.at[slot_of(a)]
        return remote(source.at[:, columns], column.at[slot_of(a), :, columns],
                      column_send.at[slot_of(a), h], column_recv.at[slot_of(a), h], at(g, to, c))

    def plane_key_copy(s, k):
        return remote(plane_key.at[0, 0], plane_key.at[s, k],
                      plane_key_send.at[s, k], plane_key_recv.at[s, k], at(group_up(s), z, core(k)))

    def column_key_copy(s, a):
        return remote(plane_key.at[0, 0], column_key.at[slot_of(a)],
                      column_key_send.at[s], column_key_recv.at[slot_of(a)], at(g, layer_up(s), c))

    def plane_res_copy(s, k):
        return remote(plane_res.at[s, k], plane_got.at[s, k],
                      plane_res_send.at[s, k], plane_res_recv.at[s, k], at(group_down(s), z, core(k)))

    def column_res_copy(a, giver):
        return remote(column_res.at[slot_of(a)], column_got.at[giver],
                      column_res_send.at[slot_of(a)], column_res_recv.at[giver], at(g, a, c))

    loads = [
        pltpu.make_async_copy(src, dst, load_sem.at[i])
        for i, (src, dst) in enumerate(
            [(embeds_hbm, embeds_ref), (cluster_hbm, cluster_ref), (priority_hbm, priority_ref)]
        )
    ]
    for load in loads:
        load.start()

    barrier = pltpu.get_barrier_semaphore()

    def greet(device):
        pl.semaphore_signal(barrier, inc=1, device_id=device, device_id_type=MESH)

    each(1, layers, lambda s: greet(at(g, layer_up(s), c)))
    for s, k in peers:
        greet(at(group_up(s), z, core(k)))

    pl.semaphore_wait(barrier, len(peers) + layers - 1)

    def first_half(s):
        return 0 if s < lows else 1

    for i in range(2):
        pl.when((z != mid) & ((z == 0) | (z == layers - 1) if i else True))(lambda: column_copy(z, i, True).start())
        for s in near:
            plane_copy(s, first_half(s) if i == 0 else 1 - first_half(s)).start()
    pass_copy(0).start()

    total[...] = jnp.full(total.shape, -1.0, jnp.float32)
    plane_key[0, 0] = jnp.full((8, lanes), -1.0, jnp.float32)
    for load in loads:
        load.wait()
    values = embeds_ref[...].astype(jnp.float32)
    scale = lax.rsqrt(jnp.sum(values * values, axis=1, keepdims=True) + 1e-06)
    normal[0, 0] = (values * scale).astype(jnp.bfloat16)
    plane_key[0, 0, 0:1, :items] = cluster_ref[...].reshape(1, items).astype(jnp.float32)
    plane_key[0, 0, 1:2, :items] = priority_ref[...].reshape(1, items).astype(jnp.float32)
    plane_key[0, 0, 2:3, :items] = jnp.broadcast_to(scale, (items, LANES)).T[0:1]
    for s, k in peers:
        plane_key_copy(s, k).start()
    each_if(1, layers, lambda s: gives(layer_up(s)), lambda s: column_key_copy(s, z).start())

    for s in near:
        plane_copy(s, first_half(s)).wait_recv()
        for t in far:
            if s == t % lows:
                relay_copy(t, 0).start()
            if s == t - t % lows:
                relay_copy(t, 1).start()

    def column_keys(key):
        key = key.T[:items]
        return key[:, 0:1], key[:, 1:2], key[:, 2:3]

    def lane_keys(blocks, i):
        return jnp.concatenate([plane_key[s, k, i:i + 1, :items] for s, k in blocks], axis=1)

    def product(rows, others):
        return lax.dot_general(
            rows, others, (((1,), (1,)), ((), ())), preferred_element_type=jnp.float32
        )

    def scaled(rows, scale):
        return (rows.astype(jnp.float32) * scale).astype(jnp.bfloat16)

    def scale_plane(s, k):
        normal[s, k] = scaled(plane[s, k], column_keys(plane_key[s, k])[2])

    def meet(rows, key, store, both):
        scores = product(rows, normal[...].reshape(len(every) * items, width))
        cluster, rank, _ = column_keys(key)
        plane_cluster, plane_rank = lane_keys(every, 0), lane_keys(every, 1)
        scores = jnp.where(cluster == plane_cluster, scores, -1.0)
        earlier = plane_rank < rank
        ahead = jnp.where(earlier, scores, -1.0)
        fold = ahead[:, :LANES]
        for start in range(LANES, ahead.shape[1], LANES):
            fold = jnp.maximum(fold, ahead[:, start:start + LANES])
        store(jnp.max(fold.T, axis=0, keepdims=True))
        if both:
            best = jnp.max(jnp.where(earlier, -1.0, scores), axis=0, keepdims=True)
            total[0:1] = jnp.maximum(total[0:1], best)

    def hand_on(a, h):
        column_copy(a, h, False).wait_recv()
        pl.when(onward(a))(lambda: column_copy(a, h, False).start())

    def meet_column(a):
        def store(best):
            column_res[slot_of(a), 0:1, :items] = best
            column_res_copy(a, z).start()

        column_key_copy(1, a).wait_recv()
        key = column_key[slot_of(a)]
        meet(scaled(column[slot_of(a)], column_keys(key)[2]), key, store, True)

    def store_own(best):
        own_res[0:1, :items] = best

    def send_plane():
        for b, (s, k) in enumerate(every):
            plane_res[s, k, 0:1, :items] = total[0:1, b * items:(b + 1) * items]
        for s, k in reversed(peers):
            plane_res_copy(s, k).start()

    def hand_on_all(a):
        for h in range(2):
            hand_on(a, h)

    pl.when(takes(0))(lambda: hand_on_all(0))
    pl.when((z > 0) & (z < layers - 1) & (z != mid))(lambda: column_copy(z, 1, True).start())
    pass_copy(0).wait_recv()
    for s, k in peers:
        plane_key_copy(s, k).wait_recv()
    scale_plane(0, 1)
    for s in near:
        plane_copy(s, 1 - first_half(s)).wait_recv()
        pass_copy(s).start()
        scale_plane(s, 0)
    for s in near:
        pass_copy(s).wait_recv()
        scale_plane(s, 1)
    for s in far:
        relay_copy(s, 0).wait_recv()
        relay_copy(s, 1).wait_recv()
        pass_copy(s).start()
        scale_plane(s, 0)
    for s in far:
        pass_copy(s).wait_recv()
        scale_plane(s, 1)
    pl.when(takes(0))(lambda: meet_column(0))
    each_if(1, layers, takes, hand_on_all)
    meet(normal[0, 0], plane_key[0, 0], store_own, False)
    each_if(1, layers, takes, meet_column)
    send_plane()

    best = own_res[0:1, :items]
    best = jnp.maximum(best, plane_res[0, 0, 0:1, :items])
    for s, k in peers:
        plane_res_copy(s, k).wait_recv()
        best = jnp.maximum(best, plane_got[s, k, 0:1, :items])
    total[0:1, :items] = best

    def take_column(giver):
        column_res_copy(0, giver).wait_recv()
        total[0:1, :items] = jnp.maximum(total[0:1, :items], column_got[giver, 0:1, :items])

    each_if(0, layers, gives, take_column)
    out_ref[...] = total[0:1, :items].reshape(items)

    for s in near:
        for h in range(2):
            plane_copy(s, h).wait_send()
    for s in far:
        for h in range(2):
            relay_copy(s, h).wait_send()
    for s in range(groups):
        pass_copy(s).wait_send()
    for s, k in peers:
        plane_key_copy(s, k).wait_send()
        plane_res_copy(s, k).wait_send()

    def sent(a):
        for h in range(2):
            column_copy(a, h, False).wait_send()

    pl.when(z != mid)(lambda: sent(z))
    each_if(0, layers, lambda a: takes(a) & onward(a), sent)
    each_if(1, layers, lambda s: gives(layer_up(s)), lambda s: column_key_copy(s, z).wait_send())
    each_if(0, layers, takes, lambda a: column_res_copy(a, z).wait_send())


def per_device(embeds, cluster, priority):
    groups, layers = lax.axis_size("grp"), lax.axis_size("dev") // 2
    slots = layers - 1
    items, width = embeds.shape
    lanes = -(-items // LANES) * LANES
    dma = pltpu.SemaphoreType.DMA
    some = max(slots, 1)
    return pl.pallas_call(
        functools.partial(kernel, groups, layers),
        out_shape=jax.ShapeDtypeStruct((items,), jnp.float32),
        in_specs=[pl.BlockSpec(memory_space=pltpu.HBM)] * 3,
        out_specs=pl.BlockSpec(memory_space=pltpu.VMEM),
        scratch_shapes=[
            pltpu.VMEM((items, width), jnp.bfloat16),
            pltpu.VMEM((items,), jnp.int32),
            pltpu.VMEM((items,), jnp.int32),
            pltpu.VMEM((groups, 2, items, width), jnp.bfloat16),
            pltpu.VMEM((groups, 2, items, width), jnp.bfloat16),
            pltpu.VMEM((some, items, width), jnp.bfloat16),
            pltpu.VMEM((groups, 2, 8, lanes), jnp.float32),
            pltpu.VMEM((some, 8, lanes), jnp.float32),
            pltpu.VMEM((groups, 2, 8, lanes), jnp.float32),
            pltpu.VMEM((some, 8, lanes), jnp.float32),
            pltpu.VMEM((groups, 2, 8, lanes), jnp.float32),
            pltpu.VMEM((layers, 8, lanes), jnp.float32),
            pltpu.VMEM((8, groups * 2 * items), jnp.float32),
            pltpu.VMEM((8, lanes), jnp.float32),
            dma((3,)),
            dma((groups, 2)), dma((groups, 2)),
            dma((groups, 2)), dma((groups, 2)),
            dma((groups,)), dma((groups,)),
            dma((some, 2)), dma((some, 2)),
            dma((groups, 2)), dma((groups, 2)),
            dma((layers,)), dma((some,)),
            dma((groups, 2)), dma((groups, 2)),
            dma((some,)), dma((layers,)),
        ],
        compiler_params=pltpu.CompilerParams(
            collective_id=0, has_side_effects=True, vmem_limit_bytes=40 * 1024 * 1024
        ),
    )(*[pltpu.with_memory_space_constraint(x, pltpu.HBM) for x in (embeds, cluster, priority)])


def solution(mesh):
    in_specs = (P(("grp", "dev"), None), P(("grp", "dev")), P(("grp", "dev")))
    out_specs = P(("grp", "dev"))
    return jax.shard_map(
        per_device, mesh=mesh, in_specs=in_specs, out_specs=out_specs, check_vma=False
    )
```

```python
import functools

import jax
import jax.numpy as jnp
from jax import lax
from jax.experimental import pallas as pl
from jax.experimental.pallas import tpu as pltpu
from jax.sharding import PartitionSpec as P

MESH = pl.DeviceIdType.MESH
LANES = 128


def batch_of(slots):
    return 0 if slots == 0 else 2 if slots % 2 == 0 else 1


def kernel(
    groups, layers, embeds_hbm, cluster_hbm, priority_hbm, out_ref,
    embeds_ref, cluster_ref, priority_ref,
    plane, normal, column, plane_key, column_key, plane_res, column_res, plane_got, column_got, total,
    own_res, partial, load_sem, plane_send, plane_recv, relay_send, relay_recv, pass_send, pass_recv,
    column_send, column_recv, plane_key_send, plane_key_recv, column_key_send, column_key_recv,
    plane_res_send, plane_res_recv, column_res_send, column_res_recv,
):
    items, width = embeds_ref.shape
    lanes = plane_key.shape[3]
    slots = layers // 2
    half = items // 2
    cut = width // 4 * 3
    parts = [(0, cut), (cut, width - cut)]
    lows = 2 if groups % 2 == 0 else 1
    highs = groups // lows
    batch = batch_of(slots)
    batches = slots // batch if slots else 1
    g, d = lax.axis_index("grp"), lax.axis_index("dev")
    z, c = d // 2, d % 2

    def at(group, layer, core):
        return {"grp": group, "dev": layer * 2 + core}

    def group_up(s):
        high, low = s // lows, s % lows
        return (g // lows + high) % highs * lows + (g % lows + low) % lows

    def group_down(s):
        high, low = s // lows, s % lows
        return (g // lows + highs - high) % highs * lows + (g % lows + lows - low) % lows

    def layer_up(s):
        return (z + s) % layers

    def core(k):
        return (c + k) % 2

    def sends(s):
        return (s % 2 == 1) & (z + s < layers) | (s % 2 == 0) & (z + s >= layers)

    def takes(s):
        return (s % 2 == 1) & (z >= s) | (s % 2 == 0) & (z < s)

    def first_even(layer):
        return layer + 2 - layer % 2

    def slot_of(s):
        to = layer_up(s)
        return (s % 2) * (s // 2) + (1 - s % 2) * ((to + 1) // 2 + (s - first_even(to)) // 2)

    def offset_of(j):
        return jnp.where(j < (z + 1) // 2, 2 * j + 1, first_even(z) + 2 * (j - (z + 1) // 2))

    def filled(j):
        return j < (z + 1) // 2 + (layers + 1 - first_even(z)) // 2

    def remote(src, dst, send, recv, device):
        return pltpu.make_async_remote_copy(
            src_ref=src, dst_ref=dst, send_sem=send, recv_sem=recv,
            device_id=device, device_id_type=MESH,
        )

    def each(start, count, body):
        if count <= 4:
            for i in range(start, count):
                body(i)
        else:
            lax.fori_loop(start, count, lambda i, carry: (body(i), carry)[1], 0)

    def each_if(start, count, test, body):
        each(start, count, lambda i: pl.when(test(i))(lambda: body(i)))

    near = [s for s in range(1, groups) if s < lows or s % lows == 0]
    far = [s for s in range(1, groups) if s not in near]
    every = [(s, k) for s in range(groups) for k in range(2)]
    peers = every[1:]

    def rows_of(h):
        return pl.ds(h * half, half)

    def plane_copy(s, h):
        return remote(embeds_hbm.at[rows_of(h)], plane.at[s, 0, rows_of(h)],
                      plane_send.at[s, h], plane_recv.at[s, h], at(group_up(s), z, c))

    def relay_copy(s, h):
        low, high = s % lows, s - s % lows
        source, way = (low, high) if h == 0 else (high, low)
        return remote(plane.at[source, 0, rows_of(h)], plane.at[s, 0, rows_of(h)],
                      relay_send.at[s, h], relay_recv.at[s, h], at(group_up(way), z, c))

    def pass_copy(s):
        return remote(plane.at[s, 0] if s else embeds_hbm, plane.at[s, 1],
                      pass_send.at[s], pass_recv.at[s], at(g, z, core(1)))

    def column_copy(s, j, h):
        columns = pl.ds(*parts[h])
        return remote(embeds_hbm.at[:, columns], column.at[j, :, columns],
                      column_send.at[s, h], column_recv.at[j, h], at(g, layer_up(s), c))

    def plane_key_copy(s, k):
        return remote(plane_key.at[0, 0], plane_key.at[s, k],
                      plane_key_send.at[s, k], plane_key_recv.at[s, k], at(group_up(s), z, core(k)))

    def column_key_copy(s, j):
        return remote(plane_key.at[0, 0], column_key.at[j],
                      column_key_send.at[s], column_key_recv.at[j], at(g, layer_up(s), c))

    def plane_res_copy(s, k):
        return remote(plane_res.at[s, k], plane_got.at[s, k],
                      plane_res_send.at[s, k], plane_res_recv.at[s, k], at(group_down(s), z, core(k)))

    def column_res_copy(j, s):
        return remote(column_res.at[j], column_got.at[s],
                      column_res_send.at[j], column_res_recv.at[s], at(g, (z + layers - s) % layers, c))

    loads = [
        pltpu.make_async_copy(src, dst, load_sem.at[i])
        for i, (src, dst) in enumerate(
            [(embeds_hbm, embeds_ref), (cluster_hbm, cluster_ref), (priority_hbm, priority_ref)]
        )
    ]
    for load in loads:
        load.start()

    barrier = pltpu.get_barrier_semaphore()

    def greet(device):
        pl.semaphore_signal(barrier, inc=1, device_id=device, device_id_type=MESH)

    column_key[...] = jnp.full(column_key.shape, -2.0, jnp.float32)
    each(1, layers, lambda s: greet(at(g, layer_up(s), c)))
    for s, k in peers:
        greet(at(group_up(s), z, core(k)))

    pl.semaphore_wait(barrier, len(peers) + layers - 1)

    def first_half(s):
        return 0 if s < lows else 1

    for i in range(2):
        each_if(1, layers, sends, lambda s: column_copy(s, slot_of(s), i).start())
        for s in near:
            plane_copy(s, first_half(s) if i == 0 else 1 - first_half(s)).start()
    pass_copy(0).start()

    total[...] = jnp.full(total.shape, -1.0, jnp.float32)
    plane_key[0, 0] = jnp.full((8, lanes), -1.0, jnp.float32)
    for load in loads:
        load.wait()
    values = embeds_ref[...].astype(jnp.float32)
    scale = lax.rsqrt(jnp.sum(values * values, axis=1, keepdims=True) + 1e-06)
    normal[0, 0] = (values * scale).astype(jnp.bfloat16)
    plane_key[0, 0, 0:1, :items] = cluster_ref[...].reshape(1, items).astype(jnp.float32)
    plane_key[0, 0, 1:2, :items] = priority_ref[...].reshape(1, items).astype(jnp.float32)
    plane_key[0, 0, 2:3, :items] = jnp.broadcast_to(scale, (items, LANES)).T[0:1]
    for s, k in peers:
        plane_key_copy(s, k).start()
    each_if(1, layers, sends, lambda s: column_key_copy(s, slot_of(s)).start())

    for s in near:
        plane_copy(s, first_half(s)).wait_recv()
        for t in far:
            if s == t % lows:
                relay_copy(t, 0).start()
            if s == t - t % lows:
                relay_copy(t, 1).start()

    def column_keys(key):
        key = key.T[:items]
        return key[:, 0:1], key[:, 1:2], key[:, 2:3]

    def lane_keys(blocks, i):
        return jnp.concatenate([plane_key[s, k, i:i + 1, :items] for s, k in blocks], axis=1)

    def product(rows, others):
        return lax.dot_general(
            rows, others, (((1,), (1,)), ((), ())), preferred_element_type=jnp.float32
        )

    def scaled(rows, scale):
        return (rows.astype(jnp.float32) * scale).astype(jnp.bfloat16)

    def scale_plane(s, k):
        normal[s, k] = scaled(plane[s, k], column_keys(plane_key[s, k])[2])

    def arrive(j, h):
        def wait(i):
            column_copy(1, i, h).wait_recv()
            if h == 0:
                column_key_copy(1, i).wait_recv()
        for i in range(batch):
            pl.when(filled(j * batch + i))(functools.partial(wait, j * batch + i))

    def part_product(j, h, scales):
        start, size = parts[h]
        here = slice(start, start + size)
        rows = [normal[0, 0, :, here]]
        rows += [scaled(column[j * batch + i, :, here], scales[i]) for i in range(batch)]
        return product(jnp.concatenate(rows, axis=0), normal[:, :, :, here].reshape(len(every) * items, size))

    def meet(j):
        arrive(j, 0)
        keys = [column_keys(plane_key[0, 0])] + [column_keys(column_key[j * batch + i]) for i in range(batch)]
        scales = [key[2] for key in keys[1:]]
        partial[...] = part_product(j, 0, scales)
        cluster, rank = (jnp.concatenate([key[i] for key in keys], axis=0) for i in range(2))
        plane_cluster, plane_rank = lane_keys(every, 0), lane_keys(every, 1)
        arrive(j, 1)
        scores = partial[...] + part_product(j, 1, scales)
        scores = jnp.where(cluster == plane_cluster, scores, -1.0)
        earlier = plane_rank < rank
        if batch:
            behind = jnp.where(earlier[items:], -1.0, scores[items:])
            total[0:1] = jnp.maximum(total[0:1], jnp.max(behind, axis=0, keepdims=True))
        if batches == 1:
            send_plane()
        ahead = jnp.where(earlier, scores, -1.0)
        fold = ahead[:, :LANES]
        for start in range(LANES, ahead.shape[1], LANES):
            fold = jnp.maximum(fold, ahead[:, start:start + LANES])

        def best_of(i):
            return jnp.max(fold[i * items:(i + 1) * items].T, axis=0, keepdims=True)

        for i in range(batch):
            column_res[j * batch + i, 0:1, :items] = best_of(1 + i)

            def send(slot):
                column_res_copy(slot, offset_of(slot)).start()
            pl.when(filled(j * batch + i))(functools.partial(send, j * batch + i))
        own_res[0:1, :items] = best_of(0)

    def send_plane():
        for b, (s, k) in enumerate(every):
            plane_res[s, k, 0:1, :items] = total[0:1, b * items:(b + 1) * items]
        for s, k in reversed(peers):
            plane_res_copy(s, k).start()

    pass_copy(0).wait_recv()
    for s, k in peers:
        plane_key_copy(s, k).wait_recv()
    scale_plane(0, 1)
    for s in near:
        plane_copy(s, 1 - first_half(s)).wait_recv()
        pass_copy(s).start()
        scale_plane(s, 0)
    for s in near:
        pass_copy(s).wait_recv()
        scale_plane(s, 1)
    for s in far:
        relay_copy(s, 0).wait_recv()
        relay_copy(s, 1).wait_recv()
        pass_copy(s).start()
        scale_plane(s, 0)
    for s in far:
        pass_copy(s).wait_recv()
        scale_plane(s, 1)
    if batches == 1:
        meet(0)
    else:
        each(0, batches, meet)
        send_plane()

    best = own_res[0:1, :items]
    best = jnp.maximum(best, plane_res[0, 0, 0:1, :items])
    for s, k in peers:
        plane_res_copy(s, k).wait_recv()
        best = jnp.maximum(best, plane_got[s, k, 0:1, :items])
    total[0:1, :items] = best

    def take_column(s):
        column_res_copy(0, s).wait_recv()
        total[0:1, :items] = jnp.maximum(total[0:1, :items], column_got[s, 0:1, :items])

    each_if(1, layers, sends, take_column)
    out_ref[...] = total[0:1, :items].reshape(items)

    for s in near:
        for h in range(2):
            plane_copy(s, h).wait_send()
    for s in far:
        for h in range(2):
            relay_copy(s, h).wait_send()
    for s in range(groups):
        pass_copy(s).wait_send()
    for s, k in peers:
        plane_key_copy(s, k).wait_send()
        plane_res_copy(s, k).wait_send()

    def sent_out(s):
        for h in range(2):
            column_copy(s, 0, h).wait_send()
        column_key_copy(s, 0).wait_send()

    each_if(1, layers, sends, sent_out)
    each_if(0, slots, filled, lambda j: column_res_copy(j, 1).wait_send())


def per_device(embeds, cluster, priority):
    groups, layers = lax.axis_size("grp"), lax.axis_size("dev") // 2
    slots = layers // 2
    items, width = embeds.shape
    lanes = -(-items // LANES) * LANES
    batch = batch_of(slots)
    dma = pltpu.SemaphoreType.DMA
    some = max(slots, 1)
    return pl.pallas_call(
        functools.partial(kernel, groups, layers),
        out_shape=jax.ShapeDtypeStruct((items,), jnp.float32),
        in_specs=[pl.BlockSpec(memory_space=pltpu.HBM)] * 3,
        out_specs=pl.BlockSpec(memory_space=pltpu.VMEM),
        scratch_shapes=[
            pltpu.VMEM((items, width), jnp.bfloat16),
            pltpu.VMEM((items,), jnp.int32),
            pltpu.VMEM((items,), jnp.int32),
            pltpu.VMEM((groups, 2, items, width), jnp.bfloat16),
            pltpu.VMEM((groups, 2, items, width), jnp.bfloat16),
            pltpu.VMEM((some, items, width), jnp.bfloat16),
            pltpu.VMEM((groups, 2, 8, lanes), jnp.float32),
            pltpu.VMEM((some, 8, lanes), jnp.float32),
            pltpu.VMEM((groups, 2, 8, lanes), jnp.float32),
            pltpu.VMEM((some, 8, lanes), jnp.float32),
            pltpu.VMEM((groups, 2, 8, lanes), jnp.float32),
            pltpu.VMEM((layers, 8, lanes), jnp.float32),
            pltpu.VMEM((8, groups * 2 * items), jnp.float32),
            pltpu.VMEM((8, lanes), jnp.float32),
            pltpu.VMEM(((1 + batch) * items, groups * 2 * items), jnp.float32),
            dma((3,)),
            dma((groups, 2)), dma((groups, 2)),
            dma((groups, 2)), dma((groups, 2)),
            dma((groups,)), dma((groups,)),
            dma((layers, 2)), dma((some, 2)),
            dma((groups, 2)), dma((groups, 2)),
            dma((layers,)), dma((some,)),
            dma((groups, 2)), dma((groups, 2)),
            dma((some,)), dma((layers,)),
        ],
        compiler_params=pltpu.CompilerParams(
            collective_id=0, has_side_effects=True, vmem_limit_bytes=40 * 1024 * 1024
        ),
    )(*[pltpu.with_memory_space_constraint(x, pltpu.HBM) for x in (embeds, cluster, priority)])


def solution(mesh):
    in_specs = (P(("grp", "dev"), None), P(("grp", "dev")), P(("grp", "dev")))
    out_specs = P(("grp", "dev"))
    return jax.shard_map(
        per_device, mesh=mesh, in_specs=in_specs, out_specs=out_specs, check_vma=False
    )
```

```python
import functools

import jax
import jax.numpy as jnp
from jax import lax
from jax.experimental import pallas as pl
from jax.experimental.pallas import tpu as pltpu
from jax.sharding import PartitionSpec as P

MESH = pl.DeviceIdType.MESH
LANES = 128


def batch_of(slots):
    return 0 if slots == 0 else 2 if slots % 2 == 0 else 1


def kernel(
    groups, layers, embeds_hbm, cluster_hbm, priority_hbm, out_ref,
    embeds_ref, cluster_ref, priority_ref,
    plane, column, plane_key, column_key, plane_res, column_res, plane_got, column_got, total,
    own_res, partial, load_sem, plane_send, plane_recv, relay_send, relay_recv, pass_send, pass_recv,
    column_send, column_recv, plane_key_send, plane_key_recv, column_key_send, column_key_recv,
    plane_res_send, plane_res_recv, column_res_send, column_res_recv,
):
    items, width = embeds_ref.shape
    lanes = plane_key.shape[3]
    slots = layers // 2
    half = items // 2
    cut = width // 4 * 3
    parts = [(0, cut), (cut, width - cut)]
    lows = 2 if groups % 2 == 0 else 1
    highs = groups // lows
    batch = batch_of(slots)
    batches = slots // batch if slots else 1
    g, d = lax.axis_index("grp"), lax.axis_index("dev")
    z, c = d // 2, d % 2

    def at(group, layer, core):
        return {"grp": group, "dev": layer * 2 + core}

    def group_up(s):
        high, low = s // lows, s % lows
        return (g // lows + high) % highs * lows + (g % lows + low) % lows

    def group_down(s):
        high, low = s // lows, s % lows
        return (g // lows + highs - high) % highs * lows + (g % lows + lows - low) % lows

    def layer_up(s):
        return (z + s) % layers

    def core(k):
        return (c + k) % 2

    def sends(s):
        return (s % 2 == 0) & (z + s < layers) | (s % 2 == 1) & (z + s >= layers)

    def first_odd(layer):
        return layer + 1 + layer % 2

    def slot_of(s):
        to = layer_up(s)
        return (1 - s % 2) * (s // 2 - 1) + (s % 2) * (to // 2 + (s - first_odd(to)) // 2)

    def offset_of(j):
        return jnp.where(j < z // 2, 2 * (j + 1), first_odd(z) + 2 * (j - z // 2))

    def filled(j):
        return j < z // 2 + (layers + 1 - first_odd(z)) // 2

    def remote(src, dst, send, recv, device):
        return pltpu.make_async_remote_copy(
            src_ref=src, dst_ref=dst, send_sem=send, recv_sem=recv,
            device_id=device, device_id_type=MESH,
        )

    def each(start, count, body):
        if count <= 4:
            for i in range(start, count):
                body(i)
        else:
            lax.fori_loop(start, count, lambda i, carry: (body(i), carry)[1], 0)

    def each_if(start, count, test, body):
        each(start, count, lambda i: pl.when(test(i))(lambda: body(i)))

    near = [s for s in range(1, groups) if s < lows or s % lows == 0]
    far = [s for s in range(1, groups) if s not in near]
    every = [(s, k) for s in range(groups) for k in range(2)]
    peers = every[1:]

    def rows_of(h):
        return pl.ds(h * half, half)

    def plane_copy(s, h):
        return remote(plane.at[0, 0, rows_of(h)], plane.at[s, 0, rows_of(h)],
                      plane_send.at[s, h], plane_recv.at[s, h], at(group_up(s), z, c))

    def relay_copy(s, h):
        low, high = s % lows, s - s % lows
        source, way = (low, high) if h == 0 else (high, low)
        return remote(plane.at[source, 0, rows_of(h)], plane.at[s, 0, rows_of(h)],
                      relay_send.at[s, h], relay_recv.at[s, h], at(group_up(way), z, c))

    def pass_copy(s):
        return remote(plane.at[s, 0], plane.at[s, 1],
                      pass_send.at[s], pass_recv.at[s], at(g, z, core(1)))

    def column_copy(s, j, h):
        columns = pl.ds(*parts[h])
        return remote(plane.at[0, 0, :, columns], column.at[j, :, columns],
                      column_send.at[s, h], column_recv.at[j, h], at(g, layer_up(s), c))

    def plane_key_copy(s, k):
        return remote(plane_key.at[0, 0], plane_key.at[s, k],
                      plane_key_send.at[s, k], plane_key_recv.at[s, k], at(group_up(s), z, core(k)))

    def column_key_copy(s, j):
        return remote(plane_key.at[0, 0], column_key.at[j],
                      column_key_send.at[s], column_key_recv.at[j], at(g, layer_up(s), c))

    def plane_res_copy(s, k):
        return remote(plane_res.at[s, k], plane_got.at[s, k],
                      plane_res_send.at[s, k], plane_res_recv.at[s, k], at(group_down(s), z, core(k)))

    def column_res_copy(j, s):
        return remote(column_res.at[j], column_got.at[s],
                      column_res_send.at[j], column_res_recv.at[s], at(g, (z + layers - s) % layers, c))

    loads = [
        pltpu.make_async_copy(src, dst, load_sem.at[i])
        for i, (src, dst) in enumerate(
            [(embeds_hbm, embeds_ref), (cluster_hbm, cluster_ref), (priority_hbm, priority_ref)]
        )
    ]
    for load in loads:
        load.start()

    barrier = pltpu.get_barrier_semaphore()

    def greet(device):
        pl.semaphore_signal(barrier, inc=1, device_id=device, device_id_type=MESH)

    column_key[...] = jnp.full(column_key.shape, -2.0, jnp.float32)
    each(1, layers, lambda s: greet(at(g, layer_up(s), c)))
    for s, k in peers:
        greet(at(group_up(s), z, core(k)))

    total[...] = jnp.full(total.shape, -1.0, jnp.float32)
    plane_key[0, 0] = jnp.full((8, lanes), -1.0, jnp.float32)
    for load in loads:
        load.wait()
    values = embeds_ref[...].astype(jnp.float32)
    scale = lax.rsqrt(jnp.sum(values * values, axis=1, keepdims=True) + 1e-06)
    plane[0, 0] = (values * scale).astype(jnp.bfloat16)
    plane_key[0, 0, 0:1, :items] = cluster_ref[...].reshape(1, items).astype(jnp.float32)
    plane_key[0, 0, 1:2, :items] = priority_ref[...].reshape(1, items).astype(jnp.float32)

    pl.semaphore_wait(barrier, len(peers) + layers - 1)

    def first_half(s):
        return 0 if s < lows else 1

    for i in range(2):
        each_if(1, layers, sends, lambda s: column_copy(s, slot_of(s), i).start())
        for s in near:
            plane_copy(s, first_half(s) if i == 0 else 1 - first_half(s)).start()
    pass_copy(0).start()

    for s, k in peers:
        plane_key_copy(s, k).start()
    each_if(1, layers, sends, lambda s: column_key_copy(s, slot_of(s)).start())

    for s in near:
        plane_copy(s, first_half(s)).wait_recv()
        for t in far:
            if s == t % lows:
                relay_copy(t, 0).start()
            if s == t - t % lows:
                relay_copy(t, 1).start()

    def column_keys(key):
        key = key.T[:items]
        return key[:, 0:1], key[:, 1:2]

    def lane_keys(blocks, i):
        return jnp.concatenate([plane_key[s, k, i:i + 1, :items] for s, k in blocks], axis=1)

    def product(rows, others):
        return lax.dot_general(
            rows, others, (((1,), (1,)), ((), ())), preferred_element_type=jnp.float32
        )

    def arrive(j, h):
        def wait(i):
            column_copy(1, i, h).wait_recv()
            if h == 0:
                column_key_copy(1, i).wait_recv()
        for i in range(batch):
            pl.when(filled(j * batch + i))(functools.partial(wait, j * batch + i))

    def part_product(j, h):
        start, size = parts[h]
        here = slice(start, start + size)
        rows = [plane[0, 0, :, here]] + [column[j * batch + i, :, here] for i in range(batch)]
        return product(jnp.concatenate(rows, axis=0), plane[:, :, :, here].reshape(len(every) * items, size))

    def meet(j):
        arrive(j, 0)
        keys = [column_keys(plane_key[0, 0])] + [column_keys(column_key[j * batch + i]) for i in range(batch)]
        partial[...] = part_product(j, 0)
        cluster, rank = (jnp.concatenate([key[i] for key in keys], axis=0) for i in range(2))
        plane_cluster, plane_rank = lane_keys(every, 0), lane_keys(every, 1)
        arrive(j, 1)
        scores = partial[...] + part_product(j, 1)
        scores = jnp.where(cluster == plane_cluster, scores, -1.0)
        earlier = plane_rank < rank
        if batch:
            behind = jnp.where(earlier[items:], -1.0, scores[items:])
            total[0:1] = jnp.maximum(total[0:1], jnp.max(behind, axis=0, keepdims=True))
        if batches == 1:
            send_plane()
        ahead = jnp.where(earlier, scores, -1.0)
        fold = ahead[:, :LANES]
        for start in range(LANES, ahead.shape[1], LANES):
            fold = jnp.maximum(fold, ahead[:, start:start + LANES])

        def best_of(i):
            return jnp.max(fold[i * items:(i + 1) * items].T, axis=0, keepdims=True)

        for i in range(batch):
            column_res[j * batch + i, 0:1, :items] = best_of(1 + i)

            def send(slot):
                column_res_copy(slot, offset_of(slot)).start()
            pl.when(filled(j * batch + i))(functools.partial(send, j * batch + i))
        own_res[0:1, :items] = best_of(0)

    def send_plane():
        for b, (s, k) in enumerate(every):
            plane_res[s, k, 0:1, :items] = total[0:1, b * items:(b + 1) * items]
        for s, k in reversed(peers):
            plane_res_copy(s, k).start()

    pass_copy(0).wait_recv()
    for s, k in peers:
        plane_key_copy(s, k).wait_recv()
    for s in near:
        plane_copy(s, 1 - first_half(s)).wait_recv()
        pass_copy(s).start()
    for s in near:
        pass_copy(s).wait_recv()
    for s in far:
        relay_copy(s, 0).wait_recv()
        relay_copy(s, 1).wait_recv()
        pass_copy(s).start()
    for s in far:
        pass_copy(s).wait_recv()
    if batches == 1:
        meet(0)
    else:
        each(0, batches, meet)
        send_plane()

    best = own_res[0:1, :items]
    best = jnp.maximum(best, plane_res[0, 0, 0:1, :items])
    for s, k in peers:
        plane_res_copy(s, k).wait_recv()
        best = jnp.maximum(best, plane_got[s, k, 0:1, :items])
    total[0:1, :items] = best

    def take_column(s):
        column_res_copy(0, s).wait_recv()
        total[0:1, :items] = jnp.maximum(total[0:1, :items], column_got[s, 0:1, :items])

    each_if(1, layers, sends, take_column)
    out_ref[...] = total[0:1, :items].reshape(items)

    for s in near:
        for h in range(2):
            plane_copy(s, h).wait_send()
    for s in far:
        for h in range(2):
            relay_copy(s, h).wait_send()
    for s in range(groups):
        pass_copy(s).wait_send()
    for s, k in peers:
        plane_key_copy(s, k).wait_send()
        plane_res_copy(s, k).wait_send()

    def sent_out(s):
        for h in range(2):
            column_copy(s, 0, h).wait_send()
        column_key_copy(s, 0).wait_send()

    each_if(1, layers, sends, sent_out)
    each_if(0, slots, filled, lambda j: column_res_copy(j, 1).wait_send())


def per_device(embeds, cluster, priority):
    groups, layers = lax.axis_size("grp"), lax.axis_size("dev") // 2
    slots = layers // 2
    items, width = embeds.shape
    lanes = -(-items // LANES) * LANES
    batch = batch_of(slots)
    dma = pltpu.SemaphoreType.DMA
    some = max(slots, 1)
    return pl.pallas_call(
        functools.partial(kernel, groups, layers),
        out_shape=jax.ShapeDtypeStruct((items,), jnp.float32),
        in_specs=[pl.BlockSpec(memory_space=pltpu.HBM)] * 3,
        out_specs=pl.BlockSpec(memory_space=pltpu.VMEM),
        scratch_shapes=[
            pltpu.VMEM((items, width), jnp.bfloat16),
            pltpu.VMEM((items,), jnp.int32),
            pltpu.VMEM((items,), jnp.int32),
            pltpu.VMEM((groups, 2, items, width), jnp.bfloat16),
            pltpu.VMEM((some, items, width), jnp.bfloat16),
            pltpu.VMEM((groups, 2, 8, lanes), jnp.float32),
            pltpu.VMEM((some, 8, lanes), jnp.float32),
            pltpu.VMEM((groups, 2, 8, lanes), jnp.float32),
            pltpu.VMEM((some, 8, lanes), jnp.float32),
            pltpu.VMEM((groups, 2, 8, lanes), jnp.float32),
            pltpu.VMEM((layers, 8, lanes), jnp.float32),
            pltpu.VMEM((8, groups * 2 * items), jnp.float32),
            pltpu.VMEM((8, lanes), jnp.float32),
            pltpu.VMEM(((1 + batch) * items, groups * 2 * items), jnp.float32),
            dma((3,)),
            dma((groups, 2)), dma((groups, 2)),
            dma((groups, 2)), dma((groups, 2)),
            dma((groups,)), dma((groups,)),
            dma((layers, 2)), dma((some, 2)),
            dma((groups, 2)), dma((groups, 2)),
            dma((layers,)), dma((some,)),
            dma((groups, 2)), dma((groups, 2)),
            dma((some,)), dma((layers,)),
        ],
        compiler_params=pltpu.CompilerParams(
            collective_id=0, has_side_effects=True, vmem_limit_bytes=40 * 1024 * 1024
        ),
    )(*[pltpu.with_memory_space_constraint(x, pltpu.HBM) for x in (embeds, cluster, priority)])


def solution(mesh):
    in_specs = (P(("grp", "dev"), None), P(("grp", "dev")), P(("grp", "dev")))
    out_specs = P(("grp", "dev"))
    return jax.shard_map(
        per_device, mesh=mesh, in_specs=in_specs, out_specs=out_specs, check_vma=False
    )
```

```python
import functools

import jax
import jax.numpy as jnp
from jax import lax
from jax.experimental import pallas as pl
from jax.experimental.pallas import tpu as pltpu
from jax.sharding import PartitionSpec as P

MESH = pl.DeviceIdType.MESH
LANES = 128


def batch_of(slots):
    return 0 if slots == 0 else 2 if slots % 2 == 0 else 1


def kernel(
    groups, layers, embeds_hbm, cluster_hbm, priority_hbm, out_ref,
    embeds_ref, cluster_ref, priority_ref,
    plane, column, plane_key, column_key, plane_res, column_res, plane_got, column_got, total,
    own_res, partial, load_sem, plane_send, plane_recv, relay_send, relay_recv, pass_send, pass_recv,
    column_send, column_recv, plane_key_send, plane_key_recv, column_key_send, column_key_recv,
    plane_res_send, plane_res_recv, column_res_send, column_res_recv,
):
    items, width = embeds_ref.shape
    lanes = plane_key.shape[3]
    slots = layers // 2
    half = items // 2
    cut = width // 4 * 3
    parts = [(0, cut), (cut, width - cut)]
    lows = 2 if groups % 2 == 0 else 1
    highs = groups // lows
    batch = batch_of(slots)
    batches = slots // batch if slots else 1
    g, d = lax.axis_index("grp"), lax.axis_index("dev")
    z, c = d // 2, d % 2

    def at(group, layer, core):
        return {"grp": group, "dev": layer * 2 + core}

    def group_up(s):
        high, low = s // lows, s % lows
        return (g // lows + high) % highs * lows + (g % lows + low) % lows

    def group_down(s):
        high, low = s // lows, s % lows
        return (g // lows + highs - high) % highs * lows + (g % lows + lows - low) % lows

    def layer_up(s):
        return (z + s) % layers

    def core(k):
        return (c + k) % 2

    def sends(s):
        return (s % 2 == 0) & (z + s < layers) | (s % 2 == 1) & (z + s >= layers)

    def first_odd(layer):
        return layer + 1 + layer % 2

    def slot_of(s):
        to = layer_up(s)
        return (1 - s % 2) * (s // 2 - 1) + (s % 2) * (to // 2 + (s - first_odd(to)) // 2)

    def offset_of(j):
        return jnp.where(j < z // 2, 2 * (j + 1), first_odd(z) + 2 * (j - z // 2))

    def filled(j):
        return j < z // 2 + (layers + 1 - first_odd(z)) // 2

    def remote(src, dst, send, recv, device):
        return pltpu.make_async_remote_copy(
            src_ref=src, dst_ref=dst, send_sem=send, recv_sem=recv,
            device_id=device, device_id_type=MESH,
        )

    def each(start, count, body):
        if count <= 4:
            for i in range(start, count):
                body(i)
        else:
            lax.fori_loop(start, count, lambda i, carry: (body(i), carry)[1], 0)

    def each_if(start, count, test, body):
        each(start, count, lambda i: pl.when(test(i))(lambda: body(i)))

    near = [s for s in range(1, groups) if s < lows or s % lows == 0]
    far = [s for s in range(1, groups) if s not in near]
    every = [(s, k) for s in range(groups) for k in range(2)]
    peers = every[1:]

    def rows_of(h):
        return pl.ds(h * half, half)

    def plane_copy(s, h):
        return remote(plane.at[0, 0, rows_of(h)], plane.at[s, 0, rows_of(h)],
                      plane_send.at[s, h], plane_recv.at[s, h], at(group_up(s), z, c))

    def relay_copy(s, h):
        low, high = s % lows, s - s % lows
        source, way = (low, high) if h == 0 else (high, low)
        return remote(plane.at[source, 0, rows_of(h)], plane.at[s, 0, rows_of(h)],
                      relay_send.at[s, h], relay_recv.at[s, h], at(group_up(way), z, c))

    def pass_copy(s):
        return remote(plane.at[s, 0], plane.at[s, 1],
                      pass_send.at[s], pass_recv.at[s], at(g, z, core(1)))

    def column_copy(s, j, h):
        columns = pl.ds(*parts[h])
        return remote(plane.at[0, 0, :, columns], column.at[j, :, columns],
                      column_send.at[s, h], column_recv.at[j, h], at(g, layer_up(s), c))

    def plane_key_copy(s, k):
        return remote(plane_key.at[0, 0], plane_key.at[s, k],
                      plane_key_send.at[s, k], plane_key_recv.at[s, k], at(group_up(s), z, core(k)))

    def column_key_copy(s, j):
        return remote(plane_key.at[0, 0], column_key.at[j],
                      column_key_send.at[s], column_key_recv.at[j], at(g, layer_up(s), c))

    def plane_res_copy(s, k):
        return remote(plane_res.at[s, k], plane_got.at[s, k],
                      plane_res_send.at[s, k], plane_res_recv.at[s, k], at(group_down(s), z, core(k)))

    def column_res_copy(j, s):
        return remote(column_res.at[j], column_got.at[s],
                      column_res_send.at[j], column_res_recv.at[s], at(g, (z + layers - s) % layers, c))

    loads = [
        pltpu.make_async_copy(src, dst, load_sem.at[i])
        for i, (src, dst) in enumerate(
            [(embeds_hbm, embeds_ref), (cluster_hbm, cluster_ref), (priority_hbm, priority_ref)]
        )
    ]
    for load in loads:
        load.start()

    barrier = pltpu.get_barrier_semaphore()

    def greet(device):
        pl.semaphore_signal(barrier, inc=1, device_id=device, device_id_type=MESH)

    column_key[...] = jnp.full(column_key.shape, -2.0, jnp.float32)
    each(1, layers, lambda s: greet(at(g, layer_up(s), c)))
    for s, k in peers:
        greet(at(group_up(s), z, core(k)))

    total[...] = jnp.full(total.shape, -1.0, jnp.float32)
    plane_key[0, 0] = jnp.full((8, lanes), -1.0, jnp.float32)
    for load in loads:
        load.wait()
    values = embeds_ref[...].astype(jnp.float32)
    scale = lax.rsqrt(jnp.sum(values * values, axis=1, keepdims=True) + 1e-06)
    plane[0, 0] = (values * scale).astype(jnp.bfloat16)
    plane_key[0, 0, 0:1, :items] = cluster_ref[...].reshape(1, items).astype(jnp.float32)
    plane_key[0, 0, 1:2, :items] = priority_ref[...].reshape(1, items).astype(jnp.float32)

    pl.semaphore_wait(barrier, len(peers) + layers - 1)

    def first_half(s):
        return 0 if s < lows else 1

    each_if(1, layers, sends, lambda s: column_key_copy(s, slot_of(s)).start())
    for i in range(2):
        each_if(1, layers, sends, lambda s: column_copy(s, slot_of(s), i).start())
        for s in near:
            plane_copy(s, first_half(s) if i == 0 else 1 - first_half(s)).start()
    pass_copy(0).start()

    for s, k in peers:
        plane_key_copy(s, k).start()

    for s in near:
        plane_copy(s, first_half(s)).wait_recv()
        for t in far:
            if s == t % lows:
                relay_copy(t, 0).start()
            if s == t - t % lows:
                relay_copy(t, 1).start()

    def column_keys(key):
        key = key.T[:items]
        return key[:, 0:1], key[:, 1:2]

    def lane_keys(blocks, i):
        return jnp.concatenate([plane_key[s, k, i:i + 1, :items] for s, k in blocks], axis=1)

    def product(rows, others):
        return lax.dot_general(
            rows, others, (((1,), (1,)), ((), ())), preferred_element_type=jnp.float32
        )

    def arrive(j, h):
        def wait(i):
            column_copy(1, i, h).wait_recv()
            if h == 0:
                column_key_copy(1, i).wait_recv()
        for i in range(batch):
            pl.when(filled(j * batch + i))(functools.partial(wait, j * batch + i))

    def part_product(j, h):
        start, size = parts[h]
        here = slice(start, start + size)
        rows = [plane[0, 0, :, here]] + [column[j * batch + i, :, here] for i in range(batch)]
        return product(jnp.concatenate(rows, axis=0), plane[:, :, :, here].reshape(len(every) * items, size))

    def meet(j):
        arrive(j, 0)
        keys = [column_keys(plane_key[0, 0])] + [column_keys(column_key[j * batch + i]) for i in range(batch)]
        partial[...] = part_product(j, 0)
        cluster, rank = (jnp.concatenate([key[i] for key in keys], axis=0) for i in range(2))
        plane_cluster, plane_rank = lane_keys(every, 0), lane_keys(every, 1)
        arrive(j, 1)
        scores = partial[...] + part_product(j, 1)
        scores = jnp.where(cluster == plane_cluster, scores, -1.0)
        earlier = plane_rank < rank
        if batch:
            behind = jnp.where(earlier[items:], -1.0, scores[items:])
            total[0:1] = jnp.maximum(total[0:1], jnp.max(behind, axis=0, keepdims=True))
        if batches == 1:
            send_plane()
        ahead = jnp.where(earlier, scores, -1.0)
        fold = ahead[:, :LANES]
        for start in range(LANES, ahead.shape[1], LANES):
            fold = jnp.maximum(fold, ahead[:, start:start + LANES])

        def best_of(i):
            return jnp.max(fold[i * items:(i + 1) * items].T, axis=0, keepdims=True)

        for i in range(batch):
            column_res[j * batch + i, 0:1, :items] = best_of(1 + i)

            def send(slot):
                column_res_copy(slot, offset_of(slot)).start()
            pl.when(filled(j * batch + i))(functools.partial(send, j * batch + i))
        own_res[0:1, :items] = best_of(0)

    def send_plane():
        for b, (s, k) in enumerate(every):
            plane_res[s, k, 0:1, :items] = total[0:1, b * items:(b + 1) * items]
        for s, k in reversed(peers):
            plane_res_copy(s, k).start()

    pass_copy(0).wait_recv()
    for s, k in peers:
        plane_key_copy(s, k).wait_recv()
    for s in near:
        plane_copy(s, 1 - first_half(s)).wait_recv()
        pass_copy(s).start()
    for s in near:
        pass_copy(s).wait_recv()
    for s in far:
        relay_copy(s, 0).wait_recv()
        relay_copy(s, 1).wait_recv()
        pass_copy(s).start()
    for s in far:
        pass_copy(s).wait_recv()
    if batches == 1:
        meet(0)
    else:
        each(0, batches, meet)
        send_plane()

    best = own_res[0:1, :items]
    best = jnp.maximum(best, plane_res[0, 0, 0:1, :items])
    for s, k in peers:
        plane_res_copy(s, k).wait_recv()
        best = jnp.maximum(best, plane_got[s, k, 0:1, :items])
    total[0:1, :items] = best

    def take_column(s):
        column_res_copy(0, s).wait_recv()
        total[0:1, :items] = jnp.maximum(total[0:1, :items], column_got[s, 0:1, :items])

    each_if(1, layers, sends, take_column)
    out_ref[...] = total[0:1, :items].reshape(items)

    for s in near:
        for h in range(2):
            plane_copy(s, h).wait_send()
    for s in far:
        for h in range(2):
            relay_copy(s, h).wait_send()
    for s in range(groups):
        pass_copy(s).wait_send()
    for s, k in peers:
        plane_key_copy(s, k).wait_send()
        plane_res_copy(s, k).wait_send()

    def sent_out(s):
        for h in range(2):
            column_copy(s, 0, h).wait_send()
        column_key_copy(s, 0).wait_send()

    each_if(1, layers, sends, sent_out)
    each_if(0, slots, filled, lambda j: column_res_copy(j, 1).wait_send())


def per_device(embeds, cluster, priority):
    groups, layers = lax.axis_size("grp"), lax.axis_size("dev") // 2
    slots = layers // 2
    items, width = embeds.shape
    lanes = -(-items // LANES) * LANES
    batch = batch_of(slots)
    dma = pltpu.SemaphoreType.DMA
    some = max(slots, 1)
    return pl.pallas_call(
        functools.partial(kernel, groups, layers),
        out_shape=jax.ShapeDtypeStruct((items,), jnp.float32),
        in_specs=[pl.BlockSpec(memory_space=pltpu.HBM)] * 3,
        out_specs=pl.BlockSpec(memory_space=pltpu.VMEM),
        scratch_shapes=[
            pltpu.VMEM((items, width), jnp.bfloat16),
            pltpu.VMEM((items,), jnp.int32),
            pltpu.VMEM((items,), jnp.int32),
            pltpu.VMEM((groups, 2, items, width), jnp.bfloat16),
            pltpu.VMEM((some, items, width), jnp.bfloat16),
            pltpu.VMEM((groups, 2, 8, lanes), jnp.float32),
            pltpu.VMEM((some, 8, lanes), jnp.float32),
            pltpu.VMEM((groups, 2, 8, lanes), jnp.float32),
            pltpu.VMEM((some, 8, lanes), jnp.float32),
            pltpu.VMEM((groups, 2, 8, lanes), jnp.float32),
            pltpu.VMEM((layers, 8, lanes), jnp.float32),
            pltpu.VMEM((8, groups * 2 * items), jnp.float32),
            pltpu.VMEM((8, lanes), jnp.float32),
            pltpu.VMEM(((1 + batch) * items, groups * 2 * items), jnp.float32),
            dma((3,)),
            dma((groups, 2)), dma((groups, 2)),
            dma((groups, 2)), dma((groups, 2)),
            dma((groups,)), dma((groups,)),
            dma((layers, 2)), dma((some, 2)),
            dma((groups, 2)), dma((groups, 2)),
            dma((layers,)), dma((some,)),
            dma((groups, 2)), dma((groups, 2)),
            dma((some,)), dma((layers,)),
        ],
        compiler_params=pltpu.CompilerParams(
            collective_id=0, has_side_effects=True, vmem_limit_bytes=40 * 1024 * 1024
        ),
    )(*[pltpu.with_memory_space_constraint(x, pltpu.HBM) for x in (embeds, cluster, priority)])


def solution(mesh):
    in_specs = (P(("grp", "dev"), None), P(("grp", "dev")), P(("grp", "dev")))
    out_specs = P(("grp", "dev"))
    return jax.shard_map(
        per_device, mesh=mesh, in_specs=in_specs, out_specs=out_specs, check_vma=False
    )
```
